128 devices in a mesh: region: 32 (over y, z, core), tracer: 4 (over x).
Axes of the slice: x: 4, y: 4, z: 4, core: 2. Of those that a mesh axis runs over, the one named last changes fastest.
Arguments:
- tracers: float32 [256, 131072], P('tracer', 'region'), may hold values from -6 to 6
- transport: bfloat16 [1024, 16, 128, 128], P('region'), may hold values from -0.09375 to 0.09375
- col_slot: int32 [1024, 16], P('region'), may hold values from 0 to 47, as said below
- export_rows: int32 [32, 8], P('region'), may hold values from 0 to 31
- send_pos: int32 [32, 4, 4], replicated, may hold values from 0 to 7
- live_blocks: int32 [32], replicated, may hold values from 1 to 32, 768 in all
- inverse: bfloat16 [1024, 128, 128], P('region'), may hold values from -0.4 to 1
- vmax: float32 [256], P('tracer'), may hold values from 1 to 4
- half_sat: float32 [256], P('tracer'), may hold values from 0.1 to 3
Outputs:
- final_tracers: float32 [256, 131072], P('tracer', 'region')
The draws below stay inside these ranges and needn't reach their ends.
Inputs may be any that keep to these rules, and one draw needn't show every extreme that they name: col_slot[g, 0] is the block row's own local block; other values are local blocks (below 32) or read slots.
All inputs are finite; a program needn't handle non-finite values.
Results may differ from the reference program's by a relative error of at most 0.01.
Values may be sent and summed in bfloat16 or wider, within the bound.
No kernel may reach another device: no remote copies, remote signals or barrier semaphores. Data moves between devices by JAX's collectives and lax.ppermute only.
A program may use at most 128 MiB of HBM per device.

```python
import math
import jax
import jax.numpy as jnp
import numpy as np
from jax import lax

NTR = 256
LEVPAD = 64
LEVELS = 50
BLOCK = 128
NB = 16
RB_DEV = 32
NEIGH = 4
EXPORT_MOST = 8
SEND_MOST = 4
CYCLES = 2
NBLOCKS = 1024
ROWS = 131072
SLOTS = 48
N_REGION = 32


def draw_col_slot(key, part):
    key = jax.random.fold_in(key, 11)
    first, second, third = jax.random.split(key, 3)
    own = jax.random.randint(first, (NBLOCKS, NB), 0, RB_DEV)
    distant = jax.random.randint(second, (NBLOCKS, NB), RB_DEV, SLOTS)
    pick = jax.random.randint(third, (NBLOCKS, NB), 0, 2)
    slots = jnp.where(pick == 1, distant, own)
    self_block = jnp.arange(NBLOCKS, dtype=jnp.int32) % RB_DEV
    slots = slots.at[:, 0].set(self_block)
    slots = slots.at[0, 1].set(SLOTS - 1)
    return slots.astype(jnp.int32)


def draw_inverse(key, part):
    key = jax.random.fold_in(key, 23)
    rows_idx = jnp.arange(BLOCK)[:, None]
    cols_idx = jnp.arange(BLOCK)[None, :]
    identity = jnp.where(rows_idx == cols_idx, 1.0, 0.0).astype(jnp.float32)
    noise = jax.random.normal(key, (NBLOCKS, BLOCK, BLOCK)) * 0.6
    spread = jnp.clip(noise / math.sqrt(BLOCK), -0.35, 0.35)
    values = 0.6 * identity[None, :, :] + spread
    return values.astype(jnp.bfloat16)


def place_ends(values, rng, least, high):
    shape = values.shape
    spot = [jax.random.randint(jax.random.fold_in(rng, axis), (), 0, shape[axis]) for axis in range(len(shape))]
    values = values.at[tuple(spot)].set(least)
    longest = shape.index(max(shape))
    spot[longest] = (spot[longest] + 1) % shape[longest]
    return values.at[tuple(spot)].set(high)


def steps_of(own_key, extent, cuts, least, high):
    level = 1.0
    for dim, shards_of in cuts:
        steps = jax.random.uniform(jax.random.fold_in(jax.random.fold_in(own_key, 6), dim), (shards_of,), jnp.float32, least / len(cuts), high / len(cuts))
        level = level * jnp.repeat(jnp.exp(steps), extent[dim] // shards_of).reshape((-1,) + (1,) * (len(extent) - 1 - dim))
    return level


def length_profile(number_of, total, limit, lean):
    loads = [(1 << 20) // math.isqrt(rank ** lean) + 1 for rank in range(2, number_of + 1)]
    rest, counts = total - limit - (number_of - 1), [1] * (number_of - 1)
    while rest > 0:
        movable = [i for i in range(number_of - 1) if counts[i] < limit]
        pool, budget = sum([loads[i] for i in movable]), rest
        for i in movable:
            more = min(limit - counts[i], max(1, budget * loads[i] // pool), rest)
            counts[i] = counts[i] + more
            rest = rest - more
    return np.array([limit] + counts)


def uneven(stream_key, amount, total, most, lean):
    if amount == 2:
        one = jax.random.randint(stream_key, (), max(1, total - most), min(most, total - 1) + 1)
        return jnp.stack([one, total - one])
    tallies = jnp.asarray(length_profile(amount, total, most, lean), jnp.int32)
    couples = (amount - 1) // 2
    donor, receiver = tallies[1:1 + 2 * couples:2], tallies[2:2 + 2 * couples:2]
    room = jnp.minimum(donor - 1, most - receiver)
    shifted = jax.random.randint(jax.random.fold_in(stream_key, 1), (couples,), 0, 1 << 20) % (room + 1)
    tallies = tallies.at[1:1 + 2 * couples:2].set(donor - shifted).at[2:2 + 2 * couples:2].set(receiver + shifted)
    return tallies[jax.random.permutation(jax.random.fold_in(stream_key, 2), amount)]


def gaussian(rng, dims, scale, most, pieces=(), kind=jnp.bfloat16):
    values = scale * jax.random.normal(rng, dims, jnp.float32)
    if pieces:
        values = values * steps_of(rng, dims, pieces, -0.22, 0.18)
    return jnp.clip(values, -most, most).astype(kind)


def setup_inputs(seed: int = 0) -> dict:
    splits = jax.random.split(jax.random.key(seed), 10)
    return {
        "tracers": gaussian(splits[0], (NTR, ROWS), 1.0, 6.0, ((0, 4), (1, 32)), jnp.float32),
        "transport": gaussian(splits[1], (NBLOCKS, NB, BLOCK, BLOCK), (2 * NB * BLOCK) ** -0.5, 0.09375, ((0, 32),)),
        "col_slot": draw_col_slot(jax.random.fold_in(splits[9], 71), 0),
        "export_rows": place_ends(jax.random.randint(splits[3], (N_REGION, EXPORT_MOST), 0, RB_DEV), jax.random.fold_in(splits[3], 1), 0, RB_DEV - 1).astype(jnp.int32),
        "send_pos": place_ends(jax.random.randint(splits[4], (N_REGION, NEIGH, SEND_MOST), 0, EXPORT_MOST), jax.random.fold_in(splits[4], 1), 0, EXPORT_MOST - 1).astype(jnp.int32),
        "live_blocks": uneven(splits[5], N_REGION, NBLOCKS * 3 // 4, RB_DEV, 2).astype(jnp.int32),
        "inverse": draw_inverse(jax.random.fold_in(splits[9], 71), 0),
        "vmax": jnp.clip(jnp.exp(math.log(4.0) - 1.3862944 * jax.random.uniform(splits[7], (NTR,), jnp.float32) ** steps_of(splits[7], (NTR,), ((0, 4),), -0.2, 0.2)), 1.0, 4.0),
        "half_sat": jnp.clip(jnp.exp(math.log(3.0) - 3.4011974 * jax.random.uniform(splits[8], (NTR,), jnp.float32) ** steps_of(splits[8], (NTR,), ((0, 4),), -0.2, 0.2)), 0.1, 3.0),
    }


def reference(tracers, transport, col_slot, export_rows, send_pos, live_blocks, inverse, vmax, half_sat):
    nreg = NBLOCKS // RB_DEV
    offsets = jnp.array([-2, -1, 1, 2], dtype=jnp.int32)
    glob = jnp.arange(NBLOCKS, dtype=jnp.int32)
    region = glob // RB_DEV
    remote = jnp.maximum(col_slot - RB_DEV, 0)
    which = remote // SEND_MOST
    within = remote % SEND_MOST
    peer = (region[:, None] + offsets[which] + nreg) % nreg
    position = send_pos[region[:, None], which, within]
    offered = export_rows[peer, position]
    colg = jnp.where(col_slot < RB_DEV, region[:, None] * RB_DEV + col_slot, peer * RB_DEV + offered).astype(jnp.int32)
    rows_all = jnp.arange(ROWS, dtype=jnp.int32)
    level = rows_all % LEVPAD
    block_of = rows_all // BLOCK
    live = (block_of % RB_DEV) < live_blocks[block_of // RB_DEV]
    mask = jnp.where(jnp.logical_and(level < LEVELS, live), 1.0, 0.0).astype(jnp.float32)
    weights = (1.0 + 8.0 * jnp.arange(NTR, dtype=jnp.float32) / (NTR - 1)).astype(jnp.float32)
    light = jnp.exp(-level.astype(jnp.float32) / LEVELS)
    state = tracers
    for cycle in range(CYCLES):
        for step in range(3):
            low = state.astype(jnp.bfloat16).reshape(NTR, NBLOCKS, BLOCK)

            def one_region(reg):
                cols = lax.dynamic_slice_in_dim(colg, reg * RB_DEV, RB_DEV, 0)
                picked = jnp.take(low, cols.reshape(-1), axis=1).reshape(NTR, RB_DEV, NB, BLOCK).astype(jnp.float32)
                mats = lax.dynamic_slice_in_dim(transport, reg * RB_DEV, RB_DEV, 0).astype(jnp.float32)
                return jnp.einsum('tbsj,bsij->tbi', picked, mats)

            flux = lax.map(one_region, jnp.arange(nreg, dtype=jnp.int32))
            flux = jnp.transpose(flux, (1, 0, 2, 3)).reshape(NTR, ROWS)
            state = mask * (state + flux)
        shade = jnp.sum(weights[:, None] * state * state, axis=0) / (16.0 * NTR)
        uptake = vmax[:, None] * (light / (1.0 + shade))[None, :] * state / (half_sat[:, None] + jnp.abs(state))
        pre = (state - uptake).astype(jnp.bfloat16).reshape(NTR, NBLOCKS, BLOCK).astype(jnp.float32)
        mixed = jnp.einsum('tbj,bij->tbi', pre, inverse.astype(jnp.float32)).reshape(NTR, ROWS)
        state = mask * mixed
    return state
```

```python
import functools

import jax
import jax.numpy as jnp
from jax import lax
from jax.experimental import pallas as pl
from jax.experimental.pallas import tpu as pltpu
from jax.sharding import PartitionSpec as P

NTR = 256
LEVPAD = 64
LEVELS = 50
CYCLES = 2
OFFSETS = (-2, -1, 1, 2)

VMEM = pltpu.VMEM
SMEM = pltpu.SMEM
F32 = jnp.float32
BF16 = jnp.bfloat16


def from_behind(value, axis, distance):
    n = lax.axis_size(axis)
    route = [((i - distance) % n, i) for i in range(n)]
    return lax.ppermute(value, axis, route)


def in_vmem(value):
    return pltpu.with_memory_space_constraint(value, VMEM)


def spec(space):
    return pl.BlockSpec(memory_space=space)


def call(kernel, name, smem, vmem, outs, scratch=(), flops=0, moved=1 << 20, resident=()):
    args = list(smem) + [in_vmem(v) if i in resident else v for i, v in enumerate(vmem)]
    return pl.pallas_call(
        kernel,
        in_specs=[spec(SMEM)] * len(smem) + [spec(VMEM)] * len(vmem),
        out_specs=[spec(s) for _, s in outs],
        out_shape=[o for o, _ in outs],
        scratch_shapes=list(scratch),
        compiler_params=pltpu.CompilerParams(vmem_limit_bytes=20 << 20),
        cost_estimate=pl.CostEstimate(flops=flops, bytes_accessed=moved, transcendentals=0),
        name=name,
    )(*args)


def kept(shape, dtype):
    return (VMEM(shape, dtype), VMEM)


def sent(shape, dtype):
    return (jax.ShapeDtypeStruct(shape, dtype), VMEM)


def send_position(send_pos, regions, near, reach, which, k):
    reader = lax.rem(lax.axis_index("region") - OFFSETS[which] + regions, regions)
    return send_pos[(reader * near + which) * reach + k]


def row_mask(block, live, shape):
    level = lax.rem(lax.broadcasted_iota(jnp.int32, shape, 1), LEVPAD)
    limit = jnp.where(block < live, LEVELS, 0)
    return jnp.where(level < limit, 1.0, 0.0).astype(F32)


def first_kernel(dims, export_rows, send_pos, tracers, *sends):
    near, reach, regions, block = dims
    for which in range(near):
        for k in range(reach):
            row = export_rows[send_position(send_pos, regions, near, reach, which, k)]
            columns = pl.ds(pl.multiple_of(row * block, block), block)
            sends[which][k] = tracers[:, columns].astype(BF16)


def spread_kernel(tracers, state, low):
    blocks, _, block = state.shape
    for b in range(blocks):
        value = tracers[:, b * block : (b + 1) * block]
        state[b] = value
        low[b] = value.astype(BF16)


def table_kernel(export_rows, rest, count):
    blocks = rest.shape[0]
    exported = [export_rows[e] for e in range(export_rows.shape[0])]
    n = jnp.int32(0)
    for b in range(blocks):
        hit = exported[0] == b
        for e in exported[1:]:
            hit = jnp.logical_or(hit, e == b)
        rest[jnp.minimum(n, blocks - 1)] = jnp.int32(b)
        n = n + jnp.where(hit, 0, 1)
    last = rest[n - 1]
    for b in range(blocks):
        rest[b] = jnp.where(b < n, rest[b], last)
    count[0] = n


def fill(ext, low, halo):
    blocks = low.shape[0]
    reach = halo[0].shape[0]
    ext[:blocks] = low[...]
    for which, part in enumerate(halo):
        ext[blocks + which * reach : blocks + (which + 1) * reach] = part[...]


def flux_of(b, cols, transport, ext):
    slots = transport.shape[1]
    picked = jnp.concatenate([ext[cols[b * slots + s]] for s in range(slots)], axis=1)
    weights = jnp.concatenate([transport[b, s] for s in range(slots)], axis=1)
    return lax.dot_general(
        picked, weights, (((1,), (1,)), ((), ())), preferred_element_type=F32
    )


def tracer_weights(width):
    first = lax.axis_index("tracer") * width
    ids = (first + lax.broadcasted_iota(jnp.int32, (width, 1), 0)).astype(F32)
    return 1.0 + 8.0 * ids / (NTR - 1)


def shade_part(state, weights):
    return jnp.sum(weights * state * state, axis=0, keepdims=True)


def export_kernel(dims, shaded, *refs):
    near, reach, regions = dims
    cols, export_rows, send_pos, live = refs[:4]
    transport, low, state = refs[4:7]
    halo = refs[7 : 7 + near]
    exported = refs[7 + near]
    outs = refs[8 + near : -1]
    ext = refs[-1]
    fill(ext, low, halo)
    live_here = live[lax.axis_index("region")]
    if shaded:
        weights = tracer_weights(state.shape[1])
    for e in range(exported.shape[0]):
        b = export_rows[e]
        value = state[b] + flux_of(b, cols, transport, ext)
        value = row_mask(b, live_here, value.shape) * value
        exported[e] = value
        if shaded:
            outs[0][pl.ds(e, 1), :] = shade_part(value, weights)
    if not shaded:
        for which in range(near):
            for k in range(reach):
                p = send_position(send_pos, regions, near, reach, which, k)
                outs[which][k] = exported[p].astype(BF16)


def rest_kernel(near, group, shaded, all_rows, *refs):
    if all_rows:
        cols, live = refs[:2]
        rest = count = None
        refs = refs[2:]
    else:
        cols, live, rest, count, export_rows = refs[:5]
        refs = refs[5:]
    transport, low, state = refs[:3]
    halo = refs[3 : 3 + near]
    refs = refs[3 + near :]
    if not all_rows:
        exported = refs[0]
        refs = refs[1:]
    new_state, extra, ext = refs
    fill(ext, low, halo)
    live_here = live[lax.axis_index("region")]
    if shaded:
        weights = tracer_weights(state.shape[1])

    def put(b, value):
        new_state[b] = value
        if shaded:
            extra[pl.ds(b, 1), :] = shade_part(value, weights)
        else:
            extra[b] = value.astype(BF16)

    def several(i, carry):
        for u in range(group):
            b = i * group + u if all_rows else rest[i * group + u]
            value = state[b] + flux_of(b, cols, transport, ext)
            put(b, row_mask(b, live_here, value.shape) * value)
        return carry

    blocks = state.shape[0]
    steps = blocks // group if all_rows else lax.div(count[0] + group - 1, group)
    lax.fori_loop(0, steps, several, 0)
    if not all_rows:
        for e in range(exported.shape[0]):
            put(export_rows[e], exported[e])


def column_of(row):
    n = row.shape[1]
    there = lax.broadcasted_iota(jnp.int32, (n, n), 0) == lax.broadcasted_iota(jnp.int32, (n, n), 1)
    return jnp.sum(jnp.where(there, row, 0.0), axis=1, keepdims=True)


def mixed_block(value, shade, vmax, half_sat, inverse):
    level = lax.rem(lax.broadcasted_iota(jnp.int32, shade.shape, 1), LEVPAD)
    light = jnp.exp(-level.astype(F32) / LEVELS)
    uptake = vmax * (light / (1.0 + shade)) * value / (half_sat + jnp.abs(value))
    pre = (value - uptake).astype(BF16)
    return lax.dot_general(pre, inverse, (((1,), (1,)), ((), ())), preferred_element_type=F32)


def implicit_kernel(dims, kind, *refs):
    near, reach, regions, peers = dims
    live = refs[0]
    refs = refs[1:]
    if kind == "export":
        export_rows, send_pos = refs[:2]
        refs = refs[2:]
    state, inverse, vmax_row, half_row = refs[:4]
    parts = refs[4 : 4 + peers]
    outs = refs[4 + peers :]
    shades = parts[0][...]
    for p in parts[1:]:
        shades = shades + p[...]
    shades = shades / (16.0 * NTR)
    vmax = column_of(vmax_row[...])
    half_sat = column_of(half_row[...])
    live_here = live[lax.axis_index("region")]
    if kind == "export":
        scratch = outs[-1]
        outs = outs[:-1]
    for e in range(state.shape[0]):
        b = export_rows[e] if kind == "export" else e
        mixed = mixed_block(state[e], shades[e : e + 1], vmax, half_sat, inverse[b])
        mixed = row_mask(b, live_here, mixed.shape) * mixed
        if kind == "export":
            scratch[e] = mixed.astype(BF16)
        elif kind == "rest":
            outs[0][e] = mixed
            outs[1][e] = mixed.astype(BF16)
        else:
            block = mixed.shape[1]
            outs[0][:, e * block : (e + 1) * block] = mixed
    if kind == "export":
        for which in range(near):
            for k in range(reach):
                p = send_position(send_pos, regions, near, reach, which, k)
                outs[which][k] = scratch[p]


def on_device(
    tracers, transport, col_slot, export_rows, send_pos, live_blocks, inverse, vmax, half_sat
):
    width, rows = tracers.shape
    blocks, slots = col_slot.shape
    block = rows // blocks
    regions, near, reach = send_pos.shape
    offered = export_rows.shape[1]
    peers = lax.axis_size("tracer")
    cols = col_slot.reshape(-1)
    exports = export_rows.reshape(-1)
    positions = send_pos.reshape(-1)
    vmax_row = vmax.reshape(1, -1)
    half_row = half_sat.reshape(1, -1)
    row_flops = 2 * width * slots * block * block

    sends = [sent((reach, width, block), BF16)] * near
    ext = VMEM((blocks + near * reach, width, block), BF16)

    def exchange(parts):
        return [from_behind(p, "region", -o) for p, o in zip(parts, OFFSETS)]

    def across(part):
        return [part] + [from_behind(part, "tracer", d) for d in range(1, peers)]

    dims = (near, reach, regions)
    halo = exchange(
        call(
            functools.partial(first_kernel, dims + (block,)),
            "offer_first",
            [exports, positions],
            [tracers],
            sends,
        )
    )
    state, low = call(
        spread_kernel,
        "spread_blocks",
        [],
        [tracers],
        [kept((blocks, width, block), F32), kept((blocks, width, block), BF16)],
        flops=row_flops * blocks // 4,
    )
    rest, count = call(
        table_kernel,
        "rest_rows",
        [exports],
        [],
        [
            (jax.ShapeDtypeStruct((blocks,), jnp.int32), SMEM),
            (jax.ShapeDtypeStruct((1,), jnp.int32), SMEM),
        ],
    )
    for cycle in range(CYCLES):
        for step in range(3):
            shaded = step == 2
            if cycle == CYCLES - 1 and shaded:
                break
            extra = [sent((offered, block), F32)] if shaded else sends
            exported, *parts = call(
                functools.partial(export_kernel, dims, shaded),
                "export_step",
                [cols, exports, positions, live_blocks],
                [transport, low, state, *halo],
                [kept((offered, width, block), F32)] + extra,
                scratch=[ext],
                flops=row_flops * offered,
                resident=(0,),
            )
            arriving = across(parts[0]) if shaded else exchange(parts)
            second = (
                sent((blocks, block), F32) if shaded else kept((blocks, width, block), BF16)
            )
            state, low = call(
                functools.partial(rest_kernel, near, 4, shaded, False),
                "rest_step",
                [cols, live_blocks, rest, count, exports],
                [transport, low, state, *halo, exported],
                [kept((blocks, width, block), F32), second],
                scratch=[ext],
                flops=row_flops * blocks,
                resident=(0,),
            )
            halo = arriving
        if cycle == CYCLES - 1:
            break
        partial_shade = low
        parts = call(
            functools.partial(implicit_kernel, dims + (peers,), "export"),
            "export_mix",
            [live_blocks, exports, positions],
            [exported, inverse, vmax_row, half_row, *halo],
            sends,
            scratch=[VMEM((offered, width, block), BF16)],
            flops=row_flops * offered // slots,
            resident=(1,),
        )
        halo = exchange(parts)
        state, low = call(
            functools.partial(implicit_kernel, dims + (peers,), "rest"),
            "rest_mix",
            [live_blocks],
            [state, inverse, vmax_row, half_row, *across(partial_shade)],
            [kept((blocks, width, block), F32), kept((blocks, width, block), BF16)],
            flops=row_flops * blocks // slots,
            resident=(1,),
        )
    state, partial_shade = call(
        functools.partial(rest_kernel, near, 8, True, True),
        "last_step",
        [cols, live_blocks],
        [transport, low, state, *halo],
        [kept((blocks, width, block), F32), sent((blocks, block), F32)],
        scratch=[ext],
        flops=row_flops * blocks,
        resident=(0,),
    )
    (out,) = call(
        functools.partial(implicit_kernel, dims + (peers,), "last"),
        "last_mix",
        [live_blocks],
        [state, inverse, vmax_row, half_row, *across(partial_shade)],
        [sent((width, rows), F32)],
        flops=row_flops * blocks // slots,
        resident=(1,),
    )
    return out


def solution(mesh):
    in_specs = (
        P("tracer", "region"),
        P("region", None, None, None),
        P("region", None),
        P("region", None),
        P(),
        P(),
        P("region", None, None),
        P("tracer"),
        P("tracer"),
    )
    out_specs = P("tracer", "region")
    return jax.shard_map(
        on_device, mesh=mesh, in_specs=in_specs, out_specs=out_specs, check_vma=False
    )
```

```python
import functools

import jax
import jax.numpy as jnp
from jax import lax
from jax.experimental import pallas as pl
from jax.experimental.pallas import tpu as pltpu
from jax.sharding import PartitionSpec as P

NTR = 256
LEVPAD = 64
LEVELS = 50
CYCLES = 2
OFFSETS = (-2, -1, 1, 2)

EXPORTS, SENDS, LINKS, REST, LIVE, SPARE, TABLE = 0, 16, 48, 64, 100, 120, 136

VMEM = pltpu.VMEM
SMEM = pltpu.SMEM
F32 = jnp.float32
BF16 = jnp.bfloat16


def from_behind(value, axis, distance):
    n = lax.axis_size(axis)
    route = [((i - distance) % n, i) for i in range(n)]
    return lax.ppermute(value, axis, route)


def link_neighbour(link, region):
    chip, core = region // 2 % 2, region % 2
    return (3 * chip, 1 + core, 3 - 3 * chip, 2 - core)[link]


def offset_of(which):
    return which - 2 + which // 2


def exchange(parts):
    n = lax.axis_size("region")
    arrived = []
    for link, part in enumerate(parts):
        route = [(r, (r + offset_of(link_neighbour(link, r))) % n) for r in range(n)]
        arrived.append(lax.ppermute(part, "region", route))
    return arrived


def in_vmem(value):
    return pltpu.with_memory_space_constraint(value, VMEM)


def spec(space):
    return pl.BlockSpec(memory_space=space)


def in_hbm(value):
    return pltpu.with_memory_space_constraint(value, pltpu.HBM)


def call(kernel, name, args, outs, scratch=(), flops=0, moved=1 << 20):
    return pl.pallas_call(
        kernel,
        in_specs=[spec(s) for _, s in args],
        out_specs=[spec(s) for _, s in outs],
        out_shape=[o for o, _ in outs],
        scratch_shapes=list(scratch),
        compiler_params=pltpu.CompilerParams(vmem_limit_bytes=24 << 20),
        cost_estimate=pl.CostEstimate(flops=flops, bytes_accessed=moved, transcendentals=0),
        name=name,
    )(*[v for v, _ in args])


def kept(shape, dtype):
    return (VMEM(shape, dtype), VMEM)


def sent(shape, dtype):
    return (jax.ShapeDtypeStruct(shape, dtype), VMEM)


def whole(values, space=VMEM):
    return [(v, space) for v in values]


def row_mask(block, live, shape):
    level = lax.rem(lax.broadcasted_iota(jnp.int32, shape, 1), LEVPAD)
    limit = jnp.where(block < live, LEVELS, 0)
    return jnp.where(level < limit, 1.0, 0.0).astype(F32)


def fetch(pairs, sems):
    copies = [pltpu.make_async_copy(a, b, sems.at[i]) for i, (a, b) in enumerate(pairs)]
    for copy in copies:
        copy.start()
    return copies


def read_position(positions, link, k):
    regions = positions.shape[2]
    mine = lax.axis_index("region")
    which = link_neighbour(link, mine)
    partner = lax.rem(mine + offset_of(which) + regions, regions)
    return positions[3 - which, k, partner]


def first_kernel(block, export_rows, send_pos, tracers, *refs):
    near, reach = send_pos.shape[:2]
    sends, (exports, positions, landed, sems, block_sems) = refs[:near], refs[near:]
    small = fetch([(export_rows, exports), (send_pos, positions)], sems)
    small[0].wait()
    copies = []
    for e in range(exports.shape[1]):
        start = pl.multiple_of(exports[0, e] * block, block)
        copies.append((tracers.at[:, pl.ds(start, block)], landed.at[e]))
    copies = fetch(copies, block_sems)
    for copy in small[1:] + copies:
        copy.wait()
    for link in range(near):
        for k in range(reach):
            sends[link][k] = landed[read_position(positions, link, k)].astype(BF16)


def write_table(table, exports, positions, lives, blocks):
    offered = exports.shape[1]
    near, reach = positions.shape[:2]
    exported = [exports[0, e] for e in range(offered)]
    free = jnp.int32(0)
    places = SPARE - offered
    for e, row in enumerate(exported):
        table[EXPORTS + e] = row
        seen = jnp.bool_(False)
        place = jnp.int32(e)
        for f in reversed(range(e)):
            same = exported[f] == row
            seen = jnp.logical_or(seen, same)
            place = jnp.where(same, f, place)
        table[SPARE + e] = place
        table[places + free] = jnp.int32(e)
        free = free + jnp.where(seen, 1, 0)
    for link in range(near):
        table[LINKS + link] = link_neighbour(link, lax.axis_index("region"))
        for k in range(reach):
            table[SENDS + link * reach + k] = table[SPARE + read_position(positions, link, k)]
    table[LIVE] = lives[lax.axis_index("region")]
    n = jnp.int32(0)
    for b in range(blocks):
        hit = exported[0] == b
        for row in exported[1:]:
            hit = jnp.logical_or(hit, row == b)
        fills = EXPORTS + table[places + jnp.minimum(n, offered - 1)]
        place = jnp.where(n < free, fills, REST + n - free)
        table[jnp.where(hit, TABLE - 1, place)] = jnp.int32(b)
        n = n + jnp.where(hit, 0, 1)


def prepare_kernel(
    export_rows,
    send_pos,
    live,
    col_slot,
    tracers,
    transport,
    state,
    low,
    early,
    table,
    cols,
    exports,
    positions,
    lives,
    landed,
    landed_rows,
    sems,
    block_sems,
):
    blocks, slots, block, _ = transport.shape
    offered = exports.shape[1]
    small = fetch(
        [
            (export_rows, exports),
            (send_pos, positions),
            (live, lives),
            (col_slot, cols),
            (tracers, landed),
        ],
        sems,
    )
    small[0].wait()
    exported = [exports[0, e] for e in range(offered)]
    again = []
    for e in range(offered):
        seen = jnp.bool_(False)
        for f in range(e):
            seen = jnp.logical_or(seen, exported[f] == exported[e])
        again.append(seen)

    def rows_copy(e, b):
        return pltpu.make_async_copy(transport.at[b], landed_rows.at[e], block_sems.at[e])

    for e in range(offered):

        @pl.when(jnp.logical_not(again[e]))
        def _():
            rows_copy(e, exported[e]).start()

    for copy in small[1:3]:
        copy.wait()
    write_table(table, exports, positions, lives, blocks)
    for e in range(offered):

        @pl.when(again[e])
        def _():
            rows_copy(e, table[EXPORTS + e]).start()

    for copy in small[3:]:
        copy.wait()
    for b in range(blocks):
        value = landed[:, b * block : (b + 1) * block]
        state[b] = value
        low[b] = value.astype(BF16)
    for e in range(offered):
        rows_copy(e, table[EXPORTS + e]).wait()
        for s in range(slots):
            early[e, s] = landed_rows[e, s].T


def fill(ext, low, halo, table):
    blocks = low.shape[0]
    reach = halo[0].shape[0]
    ext[:blocks] = low[...]
    for link, part in enumerate(halo):
        ext[pl.ds(blocks + table[LINKS + link] * reach, reach)] = part[...]


def flux_of(b, cols, weights, ext):
    picked = jnp.concatenate([ext[cols[s, b]] for s in range(cols.shape[0])], axis=1)
    return jnp.dot(picked, weights, preferred_element_type=F32)


def stacked(rows):
    slots, block, _ = rows.shape
    return rows[...].reshape(slots * block, block)


def in_groups(count, group, one):
    def several(i, carry):
        for u in range(group):
            one(i * group + u)
        return carry

    lax.fori_loop(0, count // group, several, 0)


def tracer_weights(width):
    first = lax.axis_index("tracer") * width
    ids = (first + lax.broadcasted_iota(jnp.int32, (width, 1), 0)).astype(F32)
    return 1.0 + 8.0 * ids / (NTR - 1)


def shade_part(state, weights):
    return jnp.sum(weights * state * state, axis=0, keepdims=True)


def export_kernel(cols, table, early, low, state, *refs):
    near = len(OFFSETS)
    halo, exported, sends, ext = refs[:near], refs[near], refs[near + 1 : -1], refs[-1]
    fill(ext, low, halo, table)
    for e in range(exported.shape[0]):
        b = table[EXPORTS + e]
        value = state[b] + flux_of(b, cols, stacked(early.at[e]), ext)
        exported[e] = row_mask(b, table[LIVE], value.shape) * value
    reach = sends[0].shape[0]
    for link in range(near):
        for k in range(reach):
            sends[link][k] = exported[table[SENDS + link * reach + k]].astype(BF16)


def rest_kernel(first, cols, table, weights, low, state, *refs):
    near = len(OFFSETS)
    halo, exported, refs = refs[:near], refs[near], refs[near + 1 :]
    offered = exported.shape[0]
    rest = state.shape[0] - offered
    if first:
        early, new_state, new_low, turned, ext, landed, sems = refs

        def chunk(i):
            return pltpu.make_async_copy(weights.at[table[REST + i]], landed.at[i], sems.at[i])

        for i in range(rest):
            chunk(i).start()
    else:
        new_state, new_low, ext = refs
    fill(ext, low, halo, table)

    def put(b, value):
        new_state[b] = value
        new_low[b] = value.astype(BF16)

    for e in range(offered):
        put(table[EXPORTS + e], exported[e])
        if first:
            turned[table[EXPORTS + e]] = early[e]

    def one(i):
        b = table[REST + i]
        rows = stacked((turned if first else weights).at[b])
        value = state[b] + flux_of(b, cols, rows, ext)
        put(b, row_mask(b, table[LIVE], value.shape) * value)

    if not first:
        in_groups(rest, 8, one)
        return

    group = 2

    def turn(start):
        for i in range(group):
            b = table[REST + start + i]
            for s in range(landed.shape[1]):
                turned[b, s] = landed[start + i, s].T

    def wait(start):
        for i in range(group):
            chunk(start + i).wait()

    def several(g, carry):
        start = g * group
        wait(start + group)
        for i in range(group):
            one(start + i)
        turn(start + group)
        return carry

    wait(0)
    turn(0)
    lax.fori_loop(0, rest // group - 1, several, 0)
    for i in range(group):
        one(rest - group + i)


def whole_kernel(cols, table, turned, low, state, *refs):
    near = len(OFFSETS)
    halo, (new_state, part, ext) = refs[:near], refs[near:]
    fill(ext, low, halo, table)
    weights = tracer_weights(state.shape[1])

    def one(b):
        value = state[b] + flux_of(b, cols, stacked(turned.at[b]), ext)
        value = row_mask(b, table[LIVE], value.shape) * value
        new_state[b] = value
        part[pl.ds(b, 1), :] = shade_part(value, weights)

    in_groups(state.shape[0], 8, one)


def column_of(row):
    n = row.shape[1]
    there = lax.broadcasted_iota(jnp.int32, (n, n), 0) == lax.broadcasted_iota(jnp.int32, (n, n), 1)
    return jnp.sum(jnp.where(there, row, 0.0), axis=1, keepdims=True)


def mixed_block(value, shade, vmax, half_sat, inverse):
    level = lax.rem(lax.broadcasted_iota(jnp.int32, shade.shape, 1), LEVPAD)
    light = jnp.exp(-level.astype(F32) / LEVELS)
    uptake = vmax * (light / (1.0 + shade)) * value / (half_sat + jnp.abs(value))
    pre = (value - uptake).astype(BF16)
    return lax.dot_general(pre, inverse, (((1,), (1,)), ((), ())), preferred_element_type=F32)


def implicit_kernel(kind, peers, table, state, inverse, vmax_row, half_row, *refs):
    parts, outs = refs[:peers], refs[peers:]
    total = parts[0][...]
    for p in parts[1:]:
        total = total + p[...]
    total = total / (16.0 * NTR)
    vmax = column_of(vmax_row[...])
    half_sat = column_of(half_row[...])
    if kind == "export":
        *sends, mixes, shade = outs
        shade[...] = total
        for e in range(mixes.shape[0]):
            b = table[EXPORTS + e]
            mixed = mixed_block(state[b], shade[pl.ds(b, 1), :], vmax, half_sat, inverse[b])
            mixes[e] = (row_mask(b, table[LIVE], mixed.shape) * mixed).astype(BF16)
        reach = sends[0].shape[0]
        for link, part in enumerate(sends):
            for k in range(reach):
                part[k] = mixes[table[SENDS + link * reach + k]]
        return
    blocks, _, block = state.shape
    copies = []
    for b in range(blocks):
        mixed = mixed_block(state[b], total[b : b + 1], vmax, half_sat, inverse[b])
        mixed = row_mask(b, table[LIVE], mixed.shape) * mixed
        if kind == "rest":
            outs[0][b] = mixed
            outs[1][b] = mixed.astype(BF16)
        else:
            out, made, sems = outs
            made[:, b * block : (b + 1) * block] = mixed
            each = blocks // sems.shape[0]
            if (b + 1) % each == 0:
                part = pl.ds((b + 1 - each) * block, each * block)
                copy = pltpu.make_async_copy(made.at[:, part], out.at[:, part], sems.at[b // each])
                copy.start()
                copies.append(copy)
    for copy in copies:
        copy.wait()


def on_device(
    tracers, transport, col_slot, export_rows, send_pos, live_blocks, inverse, vmax, half_sat
):
    width, rows = tracers.shape
    blocks, slots = col_slot.shape
    block = rows // blocks
    near, reach = send_pos.shape[1:]
    offered = export_rows.shape[1]
    peers = lax.axis_size("tracer")
    row_flops = 2 * width * slots * block * block

    sends = [sent((reach, width, block), BF16)] * near
    ext = VMEM((blocks + near * reach, width, block), BF16)
    state_type = kept((blocks, width, block), F32)
    low_type = kept((blocks, width, block), BF16)

    def across(part):
        return [part] + [from_behind(part, "tracer", d) for d in range(1, peers)]

    tracers, transport = in_hbm(tracers), in_hbm(transport)
    indices = [in_hbm(export_rows), in_hbm(send_pos.transpose(1, 2, 0))]
    regions = send_pos.shape[0]
    index_scratch = [
        SMEM((1, offered), jnp.int32),
        SMEM((near, reach, regions), jnp.int32),
    ]
    halo = exchange(
        call(
            functools.partial(first_kernel, block),
            "offer_first",
            whole([*indices, tracers], pl.ANY),
            sends,
            scratch=index_scratch
            + [
                VMEM((offered, width, block), F32),
                pltpu.SemaphoreType.DMA((2,)),
                pltpu.SemaphoreType.DMA((offered,)),
            ],
        )
    )
    state, low, early, table, cols = call(
        prepare_kernel,
        "prepare",
        whole([*indices, in_hbm(live_blocks), in_hbm(col_slot.T), tracers, transport], pl.ANY),
        [
            state_type,
            low_type,
            kept((offered, slots, block, block), BF16),
            (jax.ShapeDtypeStruct((TABLE,), jnp.int32), SMEM),
            (jax.ShapeDtypeStruct((slots, blocks), jnp.int32), SMEM),
        ],
        scratch=index_scratch
        + [
            SMEM((regions,), jnp.int32),
            VMEM((width, rows), F32),
            VMEM((offered, slots, block, block), BF16),
            pltpu.SemaphoreType.DMA((5,)),
            pltpu.SemaphoreType.DMA((offered,)),
        ],
        flops=row_flops * blocks,
        moved=8 << 20,
    )
    turned = None
    landing = [
        VMEM((blocks - offered, slots, block, block), BF16),
        pltpu.SemaphoreType.DMA((blocks - offered,)),
    ]
    scalars = whole([cols, table], SMEM)
    tracer_rows = [in_vmem(inverse), vmax.reshape(1, -1), half_sat.reshape(1, -1)]
    for cycle in range(CYCLES):
        for step in range(2):
            exported, *parts = call(
                export_kernel,
                "export_step",
                scalars + whole([early, low, state, *halo]),
                [kept((offered, width, block), F32)] + sends,
                scratch=[ext],
                flops=row_flops * offered,
            )
            arriving = exchange(parts)
            first = turned is None
            state, low, *more = call(
                functools.partial(rest_kernel, first),
                "rest_step",
                scalars
                + [(transport, pl.ANY) if first else (turned, VMEM)]
                + whole([low, state, *halo, exported] + ([early] if first else [])),
                [state_type, low_type] + ([kept(transport.shape, BF16)] if first else []),
                scratch=[ext] + (landing if first else []),
                flops=row_flops * blocks,
            )
            if first:
                (turned,) = more
            halo = arriving
        state, part = call(
            whole_kernel,
            "whole_step",
            scalars + whole([turned, low, state, *halo]),
            [state_type, sent((blocks, block), F32)],
            scratch=[ext],
            flops=row_flops * blocks,
        )
        operands = [(table, SMEM)] + whole([state, *tracer_rows, *across(part)])
        if cycle == CYCLES - 1:
            (out,) = call(
                functools.partial(implicit_kernel, "last", peers),
                "last_mix",
                operands,
                [(jax.ShapeDtypeStruct((width, rows), F32), pl.ANY)],
                scratch=[VMEM((width, rows), F32), pltpu.SemaphoreType.DMA((4,))],
                flops=row_flops * blocks // slots,
            )
            return out
        halo = exchange(
            call(
                functools.partial(implicit_kernel, "export", peers),
                "export_mix",
                operands,
                sends,
                scratch=[VMEM((offered, width, block), BF16), VMEM((blocks, block), F32)],
                flops=row_flops * offered // slots,
            )
        )
        state, low = call(
            functools.partial(implicit_kernel, "rest", peers),
            "rest_mix",
            operands,
            [state_type, low_type],
            flops=row_flops * blocks // slots,
        )


def solution(mesh):
    in_specs = (
        P("tracer", "region"),
        P("region", None, None, None),
        P("region", None),
        P("region", None),
        P(),
        P(),
        P("region", None, None),
        P("tracer"),
        P("tracer"),
    )
    out_specs = P("tracer", "region")
    return jax.shard_map(
        on_device, mesh=mesh, in_specs=in_specs, out_specs=out_specs, check_vma=False
    )
```

```python
import functools

import jax
import jax.numpy as jnp
from jax import lax
from jax.experimental import pallas as pl
from jax.experimental.pallas import tpu as pltpu
from jax.sharding import PartitionSpec as P

NTR = 256
LEVPAD = 64
LEVELS = 50
CYCLES = 2
OFFSETS = (-2, -1, 1, 2)

EXPORTS, SENDS, LINKS, REST, LIVE, SPARE, TABLE = 0, 16, 48, 64, 100, 120, 136

VMEM = pltpu.VMEM
SMEM = pltpu.SMEM
F32 = jnp.float32
BF16 = jnp.bfloat16


def from_behind(value, axis, distance):
    n = lax.axis_size(axis)
    route = [((i - distance) % n, i) for i in range(n)]
    return lax.ppermute(value, axis, route)


def link_neighbour(link, region):
    chip, core = region // 2 % 2, region % 2
    return (3 * chip, 1 + core, 3 - 3 * chip, 2 - core)[link]


def offset_of(which):
    return which - 2 + which // 2


def exchange(parts):
    n = lax.axis_size("region")
    arrived = []
    for link, part in enumerate(parts):
        route = [(r, (r + offset_of(link_neighbour(link, r))) % n) for r in range(n)]
        arrived.append(lax.ppermute(part, "region", route))
    return arrived


def in_vmem(value):
    return pltpu.with_memory_space_constraint(value, VMEM)


def spec(space):
    return pl.BlockSpec(memory_space=space)


def in_hbm(value):
    return pltpu.with_memory_space_constraint(value, pltpu.HBM)


def call(kernel, name, args, outs, scratch=(), flops=0, moved=1 << 20):
    return pl.pallas_call(
        kernel,
        in_specs=[spec(s) for _, s in args],
        out_specs=[spec(s) for _, s in outs],
        out_shape=[o for o, _ in outs],
        scratch_shapes=list(scratch),
        compiler_params=pltpu.CompilerParams(vmem_limit_bytes=24 << 20),
        cost_estimate=pl.CostEstimate(flops=flops, bytes_accessed=moved, transcendentals=0),
        name=name,
    )(*[v for v, _ in args])


def kept(shape, dtype):
    return (VMEM(shape, dtype), VMEM)


def sent(shape, dtype):
    return (jax.ShapeDtypeStruct(shape, dtype), VMEM)


def whole(values, space=VMEM):
    return [(v, space) for v in values]


def row_mask(block, live, shape):
    level = lax.rem(lax.broadcasted_iota(jnp.int32, shape, 1), LEVPAD)
    limit = jnp.where(block < live, LEVELS, 0)
    return jnp.where(level < limit, 1.0, 0.0).astype(F32)


def fetch(pairs, sems):
    copies = [pltpu.make_async_copy(a, b, sems.at[i]) for i, (a, b) in enumerate(pairs)]
    for copy in copies:
        copy.start()
    return copies


def read_position(positions, link, k):
    regions = positions.shape[2]
    mine = lax.axis_index("region")
    which = link_neighbour(link, mine)
    partner = lax.rem(mine + offset_of(which) + regions, regions)
    return positions[3 - which, k, partner]


def first_kernel(block, export_rows, send_pos, tracers, *refs):
    near, reach = send_pos.shape[:2]
    sends, (exports, positions, landed, sems, block_sems) = refs[:near], refs[near:]
    small = fetch([(export_rows, exports), (send_pos, positions)], sems)
    small[0].wait()
    copies = []
    for e in range(exports.shape[1]):
        start = pl.multiple_of(exports[0, e] * block, block)
        copies.append((tracers.at[:, pl.ds(start, block)], landed.at[e]))
    copies = fetch(copies, block_sems)
    for copy in small[1:] + copies:
        copy.wait()
    for link in range(near):
        for k in range(reach):
            sends[link][k] = landed[read_position(positions, link, k)].astype(BF16)


def write_table(table, exports, positions, lives, blocks):
    offered = exports.shape[1]
    near, reach = positions.shape[:2]
    exported = [exports[0, e] for e in range(offered)]
    free = jnp.int32(0)
    places = SPARE - offered
    for e, row in enumerate(exported):
        table[EXPORTS + e] = row
        seen = jnp.bool_(False)
        place = jnp.int32(e)
        for f in reversed(range(e)):
            same = exported[f] == row
            seen = jnp.logical_or(seen, same)
            place = jnp.where(same, f, place)
        table[SPARE + e] = place
        table[places + free] = jnp.int32(e)
        free = free + jnp.where(seen, 1, 0)
    for link in range(near):
        table[LINKS + link] = link_neighbour(link, lax.axis_index("region"))
        for k in range(reach):
            table[SENDS + link * reach + k] = table[SPARE + read_position(positions, link, k)]
    table[LIVE] = lives[lax.axis_index("region")]
    n = jnp.int32(0)
    for b in range(blocks):
        hit = exported[0] == b
        for row in exported[1:]:
            hit = jnp.logical_or(hit, row == b)
        fills = EXPORTS + table[places + jnp.minimum(n, offered - 1)]
        place = jnp.where(n < free, fills, REST + n - free)
        table[jnp.where(hit, TABLE - 1, place)] = jnp.int32(b)
        n = n + jnp.where(hit, 0, 1)


def prepare_kernel(
    export_rows,
    send_pos,
    live,
    col_slot,
    tracers,
    transport,
    state,
    low,
    early,
    table,
    cols,
    exports,
    positions,
    lives,
    landed,
    landed_rows,
    sems,
    block_sems,
):
    blocks, slots, block, _ = transport.shape
    offered = exports.shape[1]
    small = fetch(
        [
            (export_rows, exports),
            (send_pos, positions),
            (live, lives),
            (col_slot, cols),
            (tracers, landed),
        ],
        sems,
    )
    small[0].wait()
    exported = [exports[0, e] for e in range(offered)]
    again = []
    for e in range(offered):
        seen = jnp.bool_(False)
        for f in range(e):
            seen = jnp.logical_or(seen, exported[f] == exported[e])
        again.append(seen)

    def rows_copy(e, b):
        return pltpu.make_async_copy(transport.at[b], landed_rows.at[e], block_sems.at[e])

    for e in range(offered):

        @pl.when(jnp.logical_not(again[e]))
        def _():
            rows_copy(e, exported[e]).start()

    for copy in small[1:3]:
        copy.wait()
    write_table(table, exports, positions, lives, blocks)
    for e in range(offered):

        @pl.when(again[e])
        def _():
            rows_copy(e, table[EXPORTS + e]).start()

    for copy in small[3:]:
        copy.wait()
    for b in range(blocks):
        value = landed[:, b * block : (b + 1) * block]
        state[b] = value
        low[b] = value.astype(BF16)
    for e in range(offered):
        rows_copy(e, table[EXPORTS + e]).wait()
        for s in range(slots):
            early[e, s] = landed_rows[e, s].T


def fill(ext, low, halo, table):
    blocks = low.shape[0]
    reach = halo[0].shape[0]
    ext[:blocks] = low[...]
    for link, part in enumerate(halo):
        ext[pl.ds(blocks + table[LINKS + link] * reach, reach)] = part[...]


def flux_of(b, cols, weights, ext):
    picked = jnp.concatenate([ext[cols[s, b]] for s in range(cols.shape[0])], axis=1)
    return jnp.dot(picked, weights, preferred_element_type=F32)


def stacked(rows):
    slots, block, _ = rows.shape
    return rows[...].reshape(slots * block, block)


def in_groups(count, group, one):
    def several(i, carry):
        for u in range(group):
            one(i * group + u)
        return carry

    lax.fori_loop(0, count // group, several, 0)


def tracer_weights(width):
    first = lax.axis_index("tracer") * width
    ids = (first + lax.broadcasted_iota(jnp.int32, (width, 1), 0)).astype(F32)
    return 1.0 + 8.0 * ids / (NTR - 1)


def shade_part(state, weights):
    return jnp.sum(weights * state * state, axis=0, keepdims=True)


def export_kernel(cols, table, early, low, state, *refs):
    near = len(OFFSETS)
    halo, exported, sends, ext = refs[:near], refs[near], refs[near + 1 : -1], refs[-1]
    fill(ext, low, halo, table)
    for e in range(exported.shape[0]):
        b = table[EXPORTS + e]
        value = state[b] + flux_of(b, cols, stacked(early.at[e]), ext)
        exported[e] = row_mask(b, table[LIVE], value.shape) * value
    reach = sends[0].shape[0]
    for link in range(near):
        for k in range(reach):
            sends[link][k] = exported[table[SENDS + link * reach + k]].astype(BF16)


def rest_kernel(first, cols, table, weights, low, state, *refs):
    near = len(OFFSETS)
    halo, exported, refs = refs[:near], refs[near], refs[near + 1 :]
    offered = exported.shape[0]
    rest = state.shape[0] - offered
    if first:
        early, new_state, new_low, turned, ext, landed, sems, *fresh = refs

        def chunk(i):
            return pltpu.make_async_copy(weights.at[table[REST + i]], landed.at[i], sems.at[i])

        for i in range(rest):
            chunk(i).start()
    else:
        new_state, new_low, ext = refs
    fill(ext, low, halo, table)

    def put(b, value):
        new_state[b] = value
        new_low[b] = value.astype(BF16)

    for e in range(offered):
        put(table[EXPORTS + e], exported[e])
        if first:
            turned[table[EXPORTS + e]] = early[e]

    def one(i, rows):
        b = table[REST + i]
        value = state[b] + flux_of(b, cols, rows, ext)
        put(b, row_mask(b, table[LIVE], value.shape) * value)

    if not first:
        in_groups(rest, 8, lambda i: one(i, stacked(weights.at[table[REST + i]])))
        return

    group = fresh[0].shape[0]

    def turn(start, there):
        for i in range(group):
            b = table[REST + start + i]
            for s in range(landed.shape[1]):
                tile = landed[start + i, s].T
                turned[b, s] = tile
                there[i, s] = tile

    def wait(start):
        for i in range(group):
            chunk(start + i).wait()

    def compute(start, there):
        for i in range(group):
            one(start + i, stacked(there.at[i]))

    def several(g, carry):
        start = 2 * g * group
        wait(start + group)
        compute(start, fresh[0])
        turn(start + group, fresh[1])
        wait(start + 2 * group)
        compute(start + group, fresh[1])
        turn(start + 2 * group, fresh[0])
        return carry

    wait(0)
    turn(0, fresh[0])
    lax.fori_loop(0, rest // group // 2 - 1, several, 0)
    wait(rest - group)
    compute(rest - 2 * group, fresh[0])
    turn(rest - group, fresh[1])
    compute(rest - group, fresh[1])


def whole_kernel(cols, table, turned, low, state, *refs):
    near = len(OFFSETS)
    halo, (new_state, part, ext) = refs[:near], refs[near:]
    fill(ext, low, halo, table)
    weights = tracer_weights(state.shape[1])

    def one(b):
        value = state[b] + flux_of(b, cols, stacked(turned.at[b]), ext)
        value = row_mask(b, table[LIVE], value.shape) * value
        new_state[b] = value
        part[pl.ds(b, 1), :] = shade_part(value, weights)

    in_groups(state.shape[0], 8, one)


def column_of(row):
    n = row.shape[1]
    there = lax.broadcasted_iota(jnp.int32, (n, n), 0) == lax.broadcasted_iota(jnp.int32, (n, n), 1)
    return jnp.sum(jnp.where(there, row, 0.0), axis=1, keepdims=True)


def mixed_block(value, shade, vmax, half_sat, inverse):
    level = lax.rem(lax.broadcasted_iota(jnp.int32, shade.shape, 1), LEVPAD)
    light = jnp.exp(-level.astype(F32) / LEVELS)
    uptake = vmax * (light / (1.0 + shade)) * value / (half_sat + jnp.abs(value))
    pre = (value - uptake).astype(BF16)
    return lax.dot_general(pre, inverse, (((1,), (1,)), ((), ())), preferred_element_type=F32)


def implicit_kernel(kind, peers, table, state, inverse, vmax_row, half_row, *refs):
    parts, outs = refs[:peers], refs[peers:]
    total = parts[0][...]
    for p in parts[1:]:
        total = total + p[...]
    total = total / (16.0 * NTR)
    vmax = column_of(vmax_row[...])
    half_sat = column_of(half_row[...])
    if kind == "export":
        *sends, mixes, shade = outs
        shade[...] = total
        for e in range(mixes.shape[0]):
            b = table[EXPORTS + e]
            mixed = mixed_block(state[b], shade[pl.ds(b, 1), :], vmax, half_sat, inverse[b])
            mixes[e] = (row_mask(b, table[LIVE], mixed.shape) * mixed).astype(BF16)
        reach = sends[0].shape[0]
        for link, part in enumerate(sends):
            for k in range(reach):
                part[k] = mixes[table[SENDS + link * reach + k]]
        return
    blocks, _, block = state.shape
    copies = []
    for b in range(blocks):
        mixed = mixed_block(state[b], total[b : b + 1], vmax, half_sat, inverse[b])
        mixed = row_mask(b, table[LIVE], mixed.shape) * mixed
        if kind == "rest":
            outs[0][b] = mixed
            outs[1][b] = mixed.astype(BF16)
        else:
            out, made, sems = outs
            made[:, b * block : (b + 1) * block] = mixed
            each = blocks // sems.shape[0]
            if (b + 1) % each == 0:
                part = pl.ds((b + 1 - each) * block, each * block)
                copy = pltpu.make_async_copy(made.at[:, part], out.at[:, part], sems.at[b // each])
                copy.start()
                copies.append(copy)
    for copy in copies:
        copy.wait()


def on_device(
    tracers, transport, col_slot, export_rows, send_pos, live_blocks, inverse, vmax, half_sat
):
    width, rows = tracers.shape
    blocks, slots = col_slot.shape
    block = rows // blocks
    near, reach = send_pos.shape[1:]
    offered = export_rows.shape[1]
    peers = lax.axis_size("tracer")
    row_flops = 2 * width * slots * block * block

    sends = [sent((reach, width, block), BF16)] * near
    ext = VMEM((blocks + near * reach, width, block), BF16)
    state_type = kept((blocks, width, block), F32)
    low_type = kept((blocks, width, block), BF16)

    def across(part):
        return [part] + [from_behind(part, "tracer", d) for d in range(1, peers)]

    tracers, transport = in_hbm(tracers), in_hbm(transport)
    indices = [in_hbm(export_rows), in_hbm(send_pos.transpose(1, 2, 0))]
    regions = send_pos.shape[0]
    index_scratch = [
        SMEM((1, offered), jnp.int32),
        SMEM((near, reach, regions), jnp.int32),
    ]
    halo = exchange(
        call(
            functools.partial(first_kernel, block),
            "offer_first",
            whole([*indices, tracers], pl.ANY),
            sends,
            scratch=index_scratch
            + [
                VMEM((offered, width, block), F32),
                pltpu.SemaphoreType.DMA((2,)),
                pltpu.SemaphoreType.DMA((offered,)),
            ],
        )
    )
    state, low, early, table, cols = call(
        prepare_kernel,
        "prepare",
        whole([*indices, in_hbm(live_blocks), in_hbm(col_slot.T), tracers, transport], pl.ANY),
        [
            state_type,
            low_type,
            kept((offered, slots, block, block), BF16),
            (SMEM((TABLE,), jnp.int32), SMEM),
            (SMEM((slots, blocks), jnp.int32), SMEM),
        ],
        scratch=index_scratch
        + [
            SMEM((regions,), jnp.int32),
            VMEM((width, rows), F32),
            VMEM((offered, slots, block, block), BF16),
            pltpu.SemaphoreType.DMA((5,)),
            pltpu.SemaphoreType.DMA((offered,)),
        ],
        flops=row_flops * blocks,
        moved=8 << 20,
    )
    turned = None
    landing = [
        VMEM((blocks - offered, slots, block, block), BF16),
        pltpu.SemaphoreType.DMA((blocks - offered,)),
        *[VMEM((2, slots, block, block), BF16)] * 2,
    ]
    scalars = whole([cols, table], SMEM)
    tracer_rows = [in_vmem(inverse), vmax.reshape(1, -1), half_sat.reshape(1, -1)]
    for cycle in range(CYCLES):
        for step in range(2):
            exported, *parts = call(
                export_kernel,
                "export_step",
                scalars + whole([early, low, state, *halo]),
                [kept((offered, width, block), F32)] + sends,
                scratch=[ext],
                flops=row_flops * offered,
            )
            arriving = exchange(parts)
            first = turned is None
            state, low, *more = call(
                functools.partial(rest_kernel, first),
                "rest_step",
                scalars
                + [(transport, pl.ANY) if first else (turned, VMEM)]
                + whole([low, state, *halo, exported] + ([early] if first else [])),
                [state_type, low_type] + ([kept(transport.shape, BF16)] if first else []),
                scratch=[ext] + (landing if first else []),
                flops=row_flops * blocks,
            )
            if first:
                (turned,) = more
            halo = arriving
        state, part = call(
            whole_kernel,
            "whole_step",
            scalars + whole([turned, low, state, *halo]),
            [state_type, sent((blocks, block), F32)],
            scratch=[ext],
            flops=row_flops * blocks,
        )
        operands = [(table, SMEM)] + whole([state, *tracer_rows, *across(part)])
        if cycle == CYCLES - 1:
            (out,) = call(
                functools.partial(implicit_kernel, "last", peers),
                "last_mix",
                operands,
                [(jax.ShapeDtypeStruct((width, rows), F32), pl.ANY)],
                scratch=[VMEM((width, rows), F32), pltpu.SemaphoreType.DMA((4,))],
                flops=row_flops * blocks // slots,
            )
            return out
        halo = exchange(
            call(
                functools.partial(implicit_kernel, "export", peers),
                "export_mix",
                operands,
                sends,
                scratch=[VMEM((offered, width, block), BF16), VMEM((blocks, block), F32)],
                flops=row_flops * offered // slots,
            )
        )
        state, low = call(
            functools.partial(implicit_kernel, "rest", peers),
            "rest_mix",
            operands,
            [state_type, low_type],
            flops=row_flops * blocks // slots,
        )


def solution(mesh):
    in_specs = (
        P("tracer", "region"),
        P("region", None, None, None),
        P("region", None),
        P("region", None),
        P(),
        P(),
        P("region", None, None),
        P("tracer"),
        P("tracer"),
    )
    out_specs = P("tracer", "region")
    return jax.shard_map(
        on_device, mesh=mesh, in_specs=in_specs, out_specs=out_specs, check_vma=False
    )
```

```python
import functools

import jax
import jax.numpy as jnp
from jax import lax
from jax.experimental import pallas as pl
from jax.experimental.pallas import tpu as pltpu
from jax.sharding import PartitionSpec as P

NTR = 256
LEVPAD = 64
LEVELS = 50
CYCLES = 2
OFFSETS = (-2, -1, 1, 2)

EXPORTS, SENDS, LINKS, REST, LIVE, COUNT, SPARE, TABLE = 0, 16, 48, 64, 100, 101, 120, 136

VMEM = pltpu.VMEM
SMEM = pltpu.SMEM
F32 = jnp.float32
BF16 = jnp.bfloat16


def from_behind(value, axis, distance):
    n = lax.axis_size(axis)
    route = [((i - distance) % n, i) for i in range(n)]
    return lax.ppermute(value, axis, route)


def link_neighbour(link, region):
    chip, core = region // 2 % 2, region % 2
    return (3 * chip, 3 - 3 * chip, 1 + core, 2 - core)[link]


def offset_of(which):
    return which - 2 + which // 2


def exchange(parts):
    n = lax.axis_size("region")
    arrived = []
    for link, part in enumerate(parts):
        route = [(r, (r + offset_of(link_neighbour(link, r))) % n) for r in range(n)]
        arrived.append(lax.ppermute(part, "region", route))
    return arrived


def in_vmem(value):
    return pltpu.with_memory_space_constraint(value, VMEM)


def spec(space):
    return pl.BlockSpec(memory_space=space)


def in_hbm(value):
    return pltpu.with_memory_space_constraint(value, pltpu.HBM)


def call(kernel, name, args, outs, scratch=(), flops=0, moved=1 << 20):
    return pl.pallas_call(
        kernel,
        in_specs=[spec(s) for _, s in args],
        out_specs=[spec(s) for _, s in outs],
        out_shape=[o for o, _ in outs],
        scratch_shapes=list(scratch),
        compiler_params=pltpu.CompilerParams(vmem_limit_bytes=24 << 20),
        cost_estimate=pl.CostEstimate(flops=flops, bytes_accessed=moved, transcendentals=0),
        name=name,
    )(*[v for v, _ in args])


def kept(shape, dtype):
    return (VMEM(shape, dtype), VMEM)


def sent(shape, dtype):
    return (jax.ShapeDtypeStruct(shape, dtype), VMEM)


def whole(values, space=VMEM):
    return [(v, space) for v in values]


def row_mask(block, live, shape):
    level = lax.rem(lax.broadcasted_iota(jnp.int32, shape, 1), LEVPAD)
    limit = jnp.where(block < live, LEVELS, 0)
    return jnp.where(level < limit, 1.0, 0.0).astype(F32)


def fetch(pairs, sems):
    copies = [pltpu.make_async_copy(a, b, sems.at[i]) for i, (a, b) in enumerate(pairs)]
    for copy in copies:
        copy.start()
    return copies


def read_position(positions, link, k):
    regions = positions.shape[2]
    mine = lax.axis_index("region")
    which = link_neighbour(link, mine)
    partner = lax.rem(mine + offset_of(which) + regions, regions)
    return positions[3 - which, k, partner]


def first_kernel(block, export_rows, send_pos, tracers, *refs):
    near, reach = send_pos.shape[:2]
    sends, (exports, positions, landed, sems) = refs[:near], refs[near:]
    for copy in fetch([(tracers, landed), (export_rows, exports), (send_pos, positions)], sems):
        copy.wait()
    for link in range(near):
        for k in range(reach):
            row = exports[0, read_position(positions, link, k)]
            columns = pl.ds(pl.multiple_of(row * block, block), block)
            sends[link][k] = landed[:, columns].astype(BF16)


def write_table(table, exports, positions, lives, blocks):
    offered = exports.shape[1]
    near, reach = positions.shape[:2]
    exported = [exports[0, e] for e in range(offered)]
    free = jnp.int32(0)
    places = SPARE - offered
    for e, row in enumerate(exported):
        table[EXPORTS + e] = row
        seen = jnp.bool_(False)
        place = jnp.int32(e)
        for f in reversed(range(e)):
            same = exported[f] == row
            seen = jnp.logical_or(seen, same)
            place = jnp.where(same, f, place)
        table[SPARE + e] = place
        table[places + free] = jnp.int32(e)
        free = free + jnp.where(seen, 1, 0)
    for link in range(near):
        table[LINKS + link] = link_neighbour(link, lax.axis_index("region"))
        for k in range(reach):
            table[SENDS + link * reach + k] = table[SPARE + read_position(positions, link, k)]
    wet = lives[lax.axis_index("region")]
    table[LIVE] = wet
    n = jnp.int32(0)
    count = jnp.int32(0)
    for b in range(blocks):
        hit = exported[0] == b
        for row in exported[1:]:
            hit = jnp.logical_or(hit, row == b)
        fills = EXPORTS + table[places + jnp.minimum(n, offered - 1)]
        place = jnp.where(n < free, fills, REST + n - free)
        table[jnp.where(hit, TABLE - 1, place)] = jnp.int32(b)
        listed = jnp.logical_and(jnp.logical_not(hit), n >= free)
        count = count + jnp.where(jnp.logical_and(listed, b < wet), 1, 0)
        n = n + jnp.where(hit, 0, 1)
    table[COUNT] = count


def prepare_kernel(
    exports,
    positions,
    live,
    col_slot,
    tracers,
    transport,
    state,
    low,
    early,
    table,
    cols,
    lives,
    landed,
    landed_rows,
    sems,
    block_sems,
):
    blocks, slots, block, _ = transport.shape
    offered = exports.shape[1]
    small = fetch([(live, lives), (col_slot, cols), (tracers, landed)], sems)
    exported = [exports[0, e] for e in range(offered)]
    again = []
    for e in range(offered):
        seen = jnp.bool_(False)
        for f in range(e):
            seen = jnp.logical_or(seen, exported[f] == exported[e])
        again.append(seen)

    def rows_copy(e, b):
        return pltpu.make_async_copy(transport.at[b], landed_rows.at[e], block_sems.at[e])

    for e in range(offered):

        @pl.when(jnp.logical_not(again[e]))
        def _():
            rows_copy(e, exported[e]).start()

    small[0].wait()
    write_table(table, exports, positions, lives, blocks)
    for e in range(offered):

        @pl.when(again[e])
        def _():
            rows_copy(e, table[EXPORTS + e]).start()

    for copy in small[1:]:
        copy.wait()
    for b in range(blocks):
        value = landed[:, b * block : (b + 1) * block]
        state[b] = value
        low[b] = value.astype(BF16)
    for e in range(offered):
        rows_copy(e, table[EXPORTS + e]).wait()
        for s in range(slots):
            early[e, s] = landed_rows[e, s].T


def fill(ext, low, halo, table):
    blocks = low.shape[0]
    reach = halo[0].shape[0]
    ext[:blocks] = low[...]
    for link, part in enumerate(halo):
        ext[pl.ds(blocks + table[LINKS + link] * reach, reach)] = part[...]


def flux_of(b, cols, weights, ext):
    picked = jnp.concatenate([ext[cols[s, b]] for s in range(cols.shape[0])], axis=1)
    return jnp.dot(picked, weights, preferred_element_type=F32)


def stacked(rows):
    slots, block, _ = rows.shape
    return rows[...].reshape(slots * block, block)


def for_rest(table, rest, one, dry):
    def group_of(size, start):
        def several(i, carry):
            for u in range(size):
                one(start + i * size + u)
            return carry

        return several

    count = table[COUNT]
    left = lax.rem(count, 8)
    eights = lax.div(count, 8) + jnp.where(left > 4, 1, 0)
    fours = jnp.where(jnp.logical_and(left > 0, left <= 4), 1, 0)
    lax.fori_loop(0, eights, group_of(8, 0), 0)
    lax.fori_loop(0, fours, group_of(4, 8 * eights), 0)

    def dry_one(i, carry):
        dry(i)
        return carry

    lax.fori_loop(8 * eights + 4 * fours, rest, dry_one, 0)


def tracer_weights(width):
    first = lax.axis_index("tracer") * width
    ids = (first + lax.broadcasted_iota(jnp.int32, (width, 1), 0)).astype(F32)
    return 1.0 + 8.0 * ids / (NTR - 1)


def shade_part(state, weights):
    return jnp.sum(weights * state * state, axis=0, keepdims=True)


def export_kernel(cols, table, early, low, state, *refs):
    near = len(OFFSETS)
    halo, exported, sends, ext = refs[:near], refs[near], refs[near + 1 : -1], refs[-1]
    fill(ext, low, halo, table)
    for e in range(exported.shape[0]):
        b = table[EXPORTS + e]
        value = state[b] + flux_of(b, cols, stacked(early.at[e]), ext)
        exported[e] = row_mask(b, table[LIVE], value.shape) * value
    reach = sends[0].shape[0]
    for link in range(near):
        for k in range(reach):
            sends[link][k] = exported[table[SENDS + link * reach + k]].astype(BF16)


def rest_kernel(first, cols, table, weights, low, state, *refs):
    near = len(OFFSETS)
    halo, exported, refs = refs[:near], refs[near], refs[near + 1 :]
    offered = exported.shape[0]
    rest = state.shape[0] - offered
    if first:
        new_state, new_low, turned, ext, landed, sems, *fresh = refs

        def chunk(i):
            return pltpu.make_async_copy(weights.at[table[REST + i]], landed.at[i], sems.at[i])

        quads = jnp.maximum(lax.div(table[COUNT] + 3, 4), 1)

        def begin(i, carry):
            chunk(i).start()
            return carry

        lax.fori_loop(0, 4 * quads, begin, 0)
    else:
        new_state, new_low, ext = refs
    fill(ext, low, halo, table)

    def put(b, value):
        new_state[b] = value
        new_low[b] = value.astype(BF16)

    for e in range(offered):
        put(table[EXPORTS + e], exported[e])

    def one(i, rows):
        b = table[REST + i]
        value = state[b] + flux_of(b, cols, rows, ext)
        put(b, row_mask(b, table[LIVE], value.shape) * value)

    def dry(i):
        put(table[REST + i], jnp.zeros(state.shape[1:], F32))

    if not first:
        for_rest(table, rest, lambda i: one(i, stacked(weights.at[i])), dry)
        return

    group = fresh[0].shape[0]

    def turn(start, there):
        for i in range(group):
            for s in range(landed.shape[1]):
                tile = landed[start + i, s].T
                turned[start + i, s] = tile
                there[i, s] = tile

    def wait(start):
        for i in range(group):
            chunk(start + i).wait()

    def compute(start, there):
        for i in range(group):
            one(start + i, stacked(there.at[i]))

    def several(g, carry):
        start = 2 * g * group
        wait(start + group)
        wait(start + 2 * group)
        compute(start, fresh[0])
        turn(start + group, fresh[1])
        compute(start + group, fresh[1])
        turn(start + 2 * group, fresh[0])
        return carry

    wait(0)
    turn(0, fresh[0])
    lax.fori_loop(0, quads - 1, several, 0)
    last = 2 * group * (quads - 1)
    wait(last + group)
    compute(last, fresh[0])
    turn(last + group, fresh[1])
    compute(last + group, fresh[1])

    def dry_one(i, carry):
        dry(i)
        return carry

    lax.fori_loop(2 * group * quads, rest, dry_one, 0)


def whole_kernel(cols, table, early, turned, low, state, *refs):
    near = len(OFFSETS)
    halo, (new_state, part, ext) = refs[:near], refs[near:]
    fill(ext, low, halo, table)
    weights = tracer_weights(state.shape[1])

    def one(b, rows):
        value = state[b] + flux_of(b, cols, rows, ext)
        value = row_mask(b, table[LIVE], value.shape) * value
        new_state[b] = value
        part[pl.ds(b, 1), :] = shade_part(value, weights)

    for e in range(early.shape[0]):
        one(table[EXPORTS + e], stacked(early.at[e]))

    def dry(i):
        b = table[REST + i]
        new_state[b] = jnp.zeros(state.shape[1:], F32)
        part[pl.ds(b, 1), :] = jnp.zeros((1, part.shape[1]), F32)

    for_rest(table, turned.shape[0], lambda i: one(table[REST + i], stacked(turned.at[i])), dry)


def column_of(row):
    n = row.shape[1]
    there = lax.broadcasted_iota(jnp.int32, (n, n), 0) == lax.broadcasted_iota(jnp.int32, (n, n), 1)
    return jnp.sum(jnp.where(there, row, 0.0), axis=1, keepdims=True)


def mixed_block(value, shade, vmax, half_sat, inverse):
    level = lax.rem(lax.broadcasted_iota(jnp.int32, shade.shape, 1), LEVPAD)
    light = jnp.exp(-level.astype(F32) / LEVELS)
    uptake = vmax * (light / (1.0 + shade)) * value / (half_sat + jnp.abs(value))
    pre = (value - uptake).astype(BF16)
    return lax.dot_general(pre, inverse, (((1,), (1,)), ((), ())), preferred_element_type=F32)


def implicit_kernel(kind, peers, table, state, inverse, vmax_row, half_row, *refs):
    parts, outs = refs[:peers], refs[peers:]
    total = parts[0][...]
    for p in parts[1:]:
        total = total + p[...]
    total = total / (16.0 * NTR)
    vmax = column_of(vmax_row[...])
    half_sat = column_of(half_row[...])
    if kind == "export":
        *sends, mixes, shade = outs
        shade[...] = total
        for e in range(mixes.shape[0]):
            b = table[EXPORTS + e]
            mixed = mixed_block(state[b], shade[pl.ds(b, 1), :], vmax, half_sat, inverse[b])
            mixes[e] = (row_mask(b, table[LIVE], mixed.shape) * mixed).astype(BF16)
        reach = sends[0].shape[0]
        for link, part in enumerate(sends):
            for k in range(reach):
                part[k] = mixes[table[SENDS + link * reach + k]]
        return
    blocks, _, block = state.shape
    copies = []
    for b in range(blocks):
        mixed = mixed_block(state[b], total[b : b + 1], vmax, half_sat, inverse[b])
        mixed = row_mask(b, table[LIVE], mixed.shape) * mixed
        if kind == "rest":
            outs[0][b] = mixed
            outs[1][b] = mixed.astype(BF16)
        else:
            out, made, sems = outs
            made[:, b * block : (b + 1) * block] = mixed
            each = blocks // sems.shape[0]
            if (b + 1) % each == 0:
                part = pl.ds((b + 1 - each) * block, each * block)
                copy = pltpu.make_async_copy(made.at[:, part], out.at[:, part], sems.at[b // each])
                copy.start()
                copies.append(copy)
    for copy in copies:
        copy.wait()


def on_device(
    tracers, transport, col_slot, export_rows, send_pos, live_blocks, inverse, vmax, half_sat
):
    width, rows = tracers.shape
    blocks, slots = col_slot.shape
    block = rows // blocks
    near, reach = send_pos.shape[1:]
    offered = export_rows.shape[1]
    peers = lax.axis_size("tracer")
    row_flops = 2 * width * slots * block * block

    sends = [sent((reach, width, block), BF16)] * near
    ext = VMEM((blocks + near * reach, width, block), BF16)
    state_type = kept((blocks, width, block), F32)
    low_type = kept((blocks, width, block), BF16)

    def across(part):
        return [part] + [from_behind(part, "tracer", d) for d in range(1, peers)]

    tracers, transport = in_hbm(tracers), in_hbm(transport)
    regions = send_pos.shape[0]
    *parts, exports, positions = call(
        functools.partial(first_kernel, block),
        "offer_first",
        whole([in_hbm(export_rows), in_hbm(send_pos.transpose(1, 2, 0)), tracers], pl.ANY),
        sends
        + [
            (SMEM((1, offered), jnp.int32), SMEM),
            (SMEM((near, reach, regions), jnp.int32), SMEM),
        ],
        scratch=[VMEM((width, rows), F32), pltpu.SemaphoreType.DMA((3,))],
    )
    halo = exchange(parts)
    state, low, early, table, cols = call(
        prepare_kernel,
        "prepare",
        whole([exports, positions], SMEM)
        + whole([in_hbm(live_blocks), in_hbm(col_slot.T), tracers, transport], pl.ANY),
        [
            state_type,
            low_type,
            kept((offered, slots, block, block), BF16),
            (SMEM((TABLE,), jnp.int32), SMEM),
            (SMEM((slots, blocks), jnp.int32), SMEM),
        ],
        scratch=[
            SMEM((regions,), jnp.int32),
            VMEM((width, rows), F32),
            VMEM((offered, slots, block, block), BF16),
            pltpu.SemaphoreType.DMA((3,)),
            pltpu.SemaphoreType.DMA((offered,)),
        ],
        flops=row_flops * blocks,
        moved=8 << 20,
    )
    turned = None
    landing = [
        VMEM((blocks - offered, slots, block, block), BF16),
        pltpu.SemaphoreType.DMA((blocks - offered,)),
        *[VMEM((2, slots, block, block), BF16)] * 2,
    ]
    scalars = whole([cols, table], SMEM)
    tracer_rows = [in_vmem(inverse), vmax.reshape(1, -1), half_sat.reshape(1, -1)]
    for cycle in range(CYCLES):
        for step in range(2):
            exported, *parts = call(
                export_kernel,
                "export_step",
                scalars + whole([early, low, state, *halo]),
                [kept((offered, width, block), F32)] + sends,
                scratch=[ext],
                flops=row_flops * offered,
            )
            arriving = exchange(parts)
            first = turned is None
            state, low, *more = call(
                functools.partial(rest_kernel, first),
                "rest_step",
                scalars
                + [(transport, pl.ANY) if first else (turned, VMEM)]
                + whole([low, state, *halo, exported]),
                [state_type, low_type]
                + ([kept((blocks - offered, *transport.shape[1:]), BF16)] if first else []),
                scratch=[ext] + (landing if first else []),
                flops=row_flops * blocks,
            )
            if first:
                (turned,) = more
            halo = arriving
        state, part = call(
            whole_kernel,
            "whole_step",
            scalars + whole([early, turned, low, state, *halo]),
            [state_type, sent((blocks, block), F32)],
            scratch=[ext],
            flops=row_flops * blocks,
        )
        operands = [(table, SMEM)] + whole([state, *tracer_rows, *across(part)])
        if cycle == CYCLES - 1:
            (out,) = call(
                functools.partial(implicit_kernel, "last", peers),
                "last_mix",
                operands,
                [(jax.ShapeDtypeStruct((width, rows), F32), pl.ANY)],
                scratch=[VMEM((width, rows), F32), pltpu.SemaphoreType.DMA((4,))],
                flops=row_flops * blocks // slots,
            )
            return out
        halo = exchange(
            call(
                functools.partial(implicit_kernel, "export", peers),
                "export_mix",
                operands,
                sends,
                scratch=[VMEM((offered, width, block), BF16), VMEM((blocks, block), F32)],
                flops=row_flops * offered // slots,
            )
        )
        state, low = call(
            functools.partial(implicit_kernel, "rest", peers),
            "rest_mix",
            operands,
            [state_type, low_type],
            flops=row_flops * blocks // slots,
        )


def solution(mesh):
    in_specs = (
        P("tracer", "region"),
        P("region", None, None, None),
        P("region", None),
        P("region", None),
        P(),
        P(),
        P("region", None, None),
        P("tracer"),
        P("tracer"),
    )
    out_specs = P("tracer", "region")
    return jax.shard_map(
        on_device, mesh=mesh, in_specs=in_specs, out_specs=out_specs, check_vma=False
    )
```

```python
import functools

import jax
import jax.numpy as jnp
from jax import lax
from jax.experimental import pallas as pl
from jax.experimental.pallas import tpu as pltpu
from jax.sharding import PartitionSpec as P

NTR = 256
LEVPAD = 64
LEVELS = 50
CYCLES = 2
OFFSETS = (-2, -1, 1, 2)

EXPORTS, SENDS, LINKS, REST, LIVE, COUNT, SPARE, TABLE = 0, 16, 48, 64, 100, 101, 120, 136

VMEM = pltpu.VMEM
SMEM = pltpu.SMEM
F32 = jnp.float32
BF16 = jnp.bfloat16


def from_behind(value, axis, distance):
    n = lax.axis_size(axis)
    route = [((i - distance) % n, i) for i in range(n)]
    return lax.ppermute(value, axis, route)


def link_neighbour(link, region):
    chip, core = region // 2 % 2, region % 2
    return (3 * chip, 3 - 3 * chip, 1 + core, 2 - core)[link]


def offset_of(which):
    return which - 2 + which // 2


def exchange(parts):
    n = lax.axis_size("region")
    arrived = []
    for link, part in enumerate(parts):
        route = [(r, (r + offset_of(link_neighbour(link, r))) % n) for r in range(n)]
        arrived.append(lax.ppermute(part, "region", route))
    return arrived


def in_vmem(value):
    return pltpu.with_memory_space_constraint(value, VMEM)


def spec(space):
    return pl.BlockSpec(memory_space=space)


def in_hbm(value):
    return pltpu.with_memory_space_constraint(value, pltpu.HBM)


def call(kernel, name, args, outs, scratch=(), flops=0, moved=1 << 20):
    return pl.pallas_call(
        kernel,
        in_specs=[spec(s) for _, s in args],
        out_specs=[spec(s) for _, s in outs],
        out_shape=[o for o, _ in outs],
        scratch_shapes=list(scratch),
        compiler_params=pltpu.CompilerParams(vmem_limit_bytes=12 << 20),
        cost_estimate=pl.CostEstimate(flops=flops, bytes_accessed=moved, transcendentals=0),
        name=name,
    )(*[v for v, _ in args])


def kept(shape, dtype):
    return (VMEM(shape, dtype), VMEM)


def sent(shape, dtype):
    return (jax.ShapeDtypeStruct(shape, dtype), VMEM)


def whole(values, space=VMEM):
    return [(v, space) for v in values]


def row_mask(block, live, shape):
    level = lax.rem(lax.broadcasted_iota(jnp.int32, shape, 1), LEVPAD)
    limit = jnp.where(block < live, LEVELS, 0)
    return jnp.where(level < limit, 1.0, 0.0).astype(F32)


def fetch(pairs, sems):
    copies = [pltpu.make_async_copy(a, b, sems.at[i]) for i, (a, b) in enumerate(pairs)]
    for copy in copies:
        copy.start()
    return copies


def read_position(positions, link, k):
    regions = positions.shape[2]
    mine = lax.axis_index("region")
    which = link_neighbour(link, mine)
    partner = lax.rem(mine + offset_of(which) + regions, regions)
    return positions[3 - which, k, partner]


def first_kernel(block, export_rows, send_pos, tracers, *refs):
    near, reach = send_pos.shape[:2]
    sends, (exports, positions, landed, sems) = refs[:near], refs[near:]
    for copy in fetch([(tracers, landed), (export_rows, exports), (send_pos, positions)], sems):
        copy.wait()
    for link in range(near):
        for k in range(reach):
            row = exports[0, read_position(positions, link, k)]
            columns = pl.ds(pl.multiple_of(row * block, block), block)
            sends[link][k] = landed[:, columns].astype(BF16)


def write_table(table, exported, again, set_of_offered, positions, wet, blocks, first, places):
    near, reach = positions.shape[:2]
    offered = len(exported)
    free = jnp.int32(0)
    for e, row in enumerate(exported):
        table[EXPORTS + e] = row
        places[jnp.minimum(free, offered - 1)] = jnp.int32(EXPORTS + e)
        free = free + again[e].astype(jnp.int32)
    for e in reversed(range(offered)):
        first[exported[e]] = jnp.int32(e)
    mine = lax.axis_index("region")
    for link in range(near):
        table[LINKS + link] = link_neighbour(link, mine)
        for k in range(reach):
            place = read_position(positions, link, k)
            table[SENDS + link * reach + k] = first[table[EXPORTS + place]]
    table[LIVE] = wet
    n = jnp.int32(0)
    count = jnp.int32(0)
    for b in range(blocks):
        other = 1 - jnp.bitwise_and(lax.shift_right_logical(set_of_offered, jnp.int32(b)), 1)
        place = jnp.where(n < free, places[jnp.minimum(n, offered - 1)], REST + n - free)
        table[jnp.where(other == 1, place, TABLE - 1)] = jnp.int32(b)
        count = count + jnp.where(b < wet, other, 0)
        n = n + other
    table[COUNT] = jnp.maximum(count - free, 0)


def prepare_kernel(
    exports,
    positions,
    live,
    col_slot,
    tracers,
    transport,
    state,
    low,
    early,
    table,
    cols,
    lives,
    first,
    places,
    sems,
):
    blocks, slots, block, _ = transport.shape
    offered = exports.shape[1]
    small = fetch([(live, lives), (col_slot, cols)], sems)
    exported = [exports[0, e] for e in range(offered)]
    again = []
    set_of_offered = jnp.int32(0)
    for row in exported:
        bit = lax.shift_left(jnp.int32(1), row)
        again.append(jnp.bitwise_and(set_of_offered, bit) != 0)
        set_of_offered = jnp.bitwise_or(set_of_offered, bit)

    small[0].wait()
    wet = lives[lax.axis_index("region")]
    write_table(table, exported, again, set_of_offered, positions, wet, blocks, first, places)
    for b in range(blocks):
        value = tracers[:, b * block : (b + 1) * block]
        state[b] = value
        low[b] = value.astype(BF16)
    for e in range(offered):
        b = table[EXPORTS + e]
        for s in range(slots):
            early[e, s] = transport[b, s].T
    small[1].wait()


def fill(ext, low, halo, table):
    blocks = low.shape[0]
    reach = halo[0].shape[0]
    ext[:blocks] = low[...]
    for link, part in enumerate(halo):
        ext[pl.ds(blocks + table[LINKS + link] * reach, reach)] = part[...]


def flux_of(b, cols, weights, ext):
    picked = jnp.concatenate([ext[cols[s, b]] for s in range(cols.shape[0])], axis=1)
    return jnp.dot(picked, weights, preferred_element_type=F32)


def stacked(rows):
    slots, block, _ = rows.shape
    return rows[...].reshape(slots * block, block)


def for_rest(table, rest, one, dry):
    def group_of(size, start):
        def several(i, carry):
            for u in range(size):
                one(start + i * size + u)
            return carry

        return several

    count = table[COUNT]
    left = lax.rem(count, 8)
    eights = lax.div(count, 8) + jnp.where(left > 4, 1, 0)
    fours = jnp.where(jnp.logical_and(left > 0, left <= 4), 1, 0)
    lax.fori_loop(0, eights, group_of(8, 0), 0)
    lax.fori_loop(0, fours, group_of(4, 8 * eights), 0)

    def dry_one(i, carry):
        dry(i)
        return carry

    lax.fori_loop(8 * eights + 4 * fours, rest, dry_one, 0)


def tracer_weights(width):
    first = lax.axis_index("tracer") * width
    ids = (first + lax.broadcasted_iota(jnp.int32, (width, 1), 0)).astype(F32)
    return 1.0 + 8.0 * ids / (NTR - 1)


def shade_part(state, weights):
    return jnp.sum(weights * state * state, axis=0, keepdims=True)


def export_kernel(cols, table, early, low, state, *refs):
    near = len(OFFSETS)
    halo, exported, sends, ext = refs[:near], refs[near], refs[near + 1 : -1], refs[-1]
    fill(ext, low, halo, table)
    for e in range(exported.shape[0]):
        b = table[EXPORTS + e]
        value = state[b] + flux_of(b, cols, stacked(early.at[e]), ext)
        exported[e] = row_mask(b, table[LIVE], value.shape) * value
    reach = sends[0].shape[0]
    for link in range(near):
        for k in range(reach):
            sends[link][k] = exported[table[SENDS + link * reach + k]].astype(BF16)


def rest_kernel(first, cols, table, weights, low, state, *refs):
    near = len(OFFSETS)
    halo, exported, refs = refs[:near], refs[near], refs[near + 1 :]
    offered = exported.shape[0]
    rest = state.shape[0] - offered
    if first:
        new_state, new_low, turned, ext, *fresh = refs
        quads = jnp.maximum(lax.div(table[COUNT] + 3, 4), 1)
    else:
        new_state, new_low, ext = refs
    fill(ext, low, halo, table)

    def put(b, value):
        new_state[b] = value
        new_low[b] = value.astype(BF16)

    for e in range(offered):
        put(table[EXPORTS + e], exported[e])

    def one(i, rows):
        b = table[REST + i]
        value = state[b] + flux_of(b, cols, rows, ext)
        put(b, row_mask(b, table[LIVE], value.shape) * value)

    def dry(i):
        put(table[REST + i], jnp.zeros(state.shape[1:], F32))

    if not first:
        for_rest(table, rest, lambda i: one(i, stacked(weights.at[i])), dry)
        return

    group = fresh[0].shape[0]

    def turn(start, there):
        for i in range(group):
            b = table[REST + start + i]
            for s in range(weights.shape[1]):
                tile = weights[b, s].T
                turned[start + i, s] = tile
                there[i, s] = tile

    def compute(start, there):
        for i in range(group):
            one(start + i, stacked(there.at[i]))

    def several(g, carry):
        start = 2 * g * group
        compute(start, fresh[0])
        turn(start + group, fresh[1])
        compute(start + group, fresh[1])
        turn(start + 2 * group, fresh[0])
        return carry

    turn(0, fresh[0])
    lax.fori_loop(0, quads - 1, several, 0)
    last = 2 * group * (quads - 1)
    compute(last, fresh[0])
    turn(last + group, fresh[1])
    compute(last + group, fresh[1])

    def dry_one(i, carry):
        dry(i)
        return carry

    lax.fori_loop(2 * group * quads, rest, dry_one, 0)


def whole_kernel(cols, table, early, turned, low, state, *refs):
    near = len(OFFSETS)
    halo, (new_state, part, ext) = refs[:near], refs[near:]
    fill(ext, low, halo, table)
    weights = tracer_weights(state.shape[1])

    def one(b, rows):
        value = state[b] + flux_of(b, cols, rows, ext)
        value = row_mask(b, table[LIVE], value.shape) * value
        new_state[b] = value
        part[pl.ds(b, 1), :] = shade_part(value, weights)

    for e in range(early.shape[0]):
        one(table[EXPORTS + e], stacked(early.at[e]))

    def dry(i):
        b = table[REST + i]
        new_state[b] = jnp.zeros(state.shape[1:], F32)
        part[pl.ds(b, 1), :] = jnp.zeros((1, part.shape[1]), F32)

    for_rest(table, turned.shape[0], lambda i: one(table[REST + i], stacked(turned.at[i])), dry)


def column_of(row):
    n = row.shape[1]
    there = lax.broadcasted_iota(jnp.int32, (n, n), 0) == lax.broadcasted_iota(jnp.int32, (n, n), 1)
    return jnp.sum(jnp.where(there, row, 0.0), axis=1, keepdims=True)


def mixed_block(value, shade, vmax, half_sat, inverse):
    level = lax.rem(lax.broadcasted_iota(jnp.int32, shade.shape, 1), LEVPAD)
    light = jnp.exp(-level.astype(F32) / LEVELS)
    uptake = vmax * (light / (1.0 + shade)) * value / (half_sat + jnp.abs(value))
    pre = (value - uptake).astype(BF16)
    return lax.dot_general(pre, inverse, (((1,), (1,)), ((), ())), preferred_element_type=F32)


def implicit_kernel(kind, peers, table, state, inverse, vmax_row, half_row, *refs):
    parts, outs = refs[:peers], refs[peers:]
    total = parts[0][...]
    for p in parts[1:]:
        total = total + p[...]
    total = total / (16.0 * NTR)
    vmax = column_of(vmax_row[...])
    half_sat = column_of(half_row[...])
    if kind == "export":
        *sends, mixes, shade = outs
        shade[...] = total
        for e in range(mixes.shape[0]):
            b = table[EXPORTS + e]
            mixed = mixed_block(state[b], shade[pl.ds(b, 1), :], vmax, half_sat, inverse[b])
            mixes[e] = (row_mask(b, table[LIVE], mixed.shape) * mixed).astype(BF16)
        reach = sends[0].shape[0]
        for link, part in enumerate(sends):
            for k in range(reach):
                part[k] = mixes[table[SENDS + link * reach + k]]
        return
    blocks, _, block = state.shape
    copies = []
    for b in range(blocks):
        mixed = mixed_block(state[b], total[b : b + 1], vmax, half_sat, inverse[b])
        mixed = row_mask(b, table[LIVE], mixed.shape) * mixed
        if kind == "rest":
            outs[0][b] = mixed
            outs[1][b] = mixed.astype(BF16)
        else:
            out, made, sems = outs
            made[:, b * block : (b + 1) * block] = mixed
            each = blocks // sems.shape[0]
            if (b + 1) % each == 0:
                part = pl.ds((b + 1 - each) * block, each * block)
                copy = pltpu.make_async_copy(made.at[:, part], out.at[:, part], sems.at[b // each])
                copy.start()
                copies.append(copy)
    for copy in copies:
        copy.wait()


def on_device(
    tracers, transport, col_slot, export_rows, send_pos, live_blocks, inverse, vmax, half_sat
):
    width, rows = tracers.shape
    blocks, slots = col_slot.shape
    block = rows // blocks
    near, reach = send_pos.shape[1:]
    offered = export_rows.shape[1]
    peers = lax.axis_size("tracer")
    row_flops = 2 * width * slots * block * block

    sends = [sent((reach, width, block), BF16)] * near
    ext = VMEM((blocks + near * reach, width, block), BF16)
    state_type = kept((blocks, width, block), F32)
    low_type = kept((blocks, width, block), BF16)

    def across(part):
        return [part] + [lax.ppermute(part, "tracer", [(i, i ^ d) for i in range(peers)]) for d in (1, 3, 2)]

    regions = send_pos.shape[0]
    *parts, exports, positions = call(
        functools.partial(first_kernel, block),
        "offer_first",
        whole([in_hbm(export_rows), in_hbm(send_pos.transpose(1, 2, 0)), in_hbm(tracers)], pl.ANY),
        sends
        + [
            (SMEM((1, offered), jnp.int32), SMEM),
            (SMEM((near, reach, regions), jnp.int32), SMEM),
        ],
        scratch=[VMEM((width, rows), F32), pltpu.SemaphoreType.DMA((3,))],
        flops=12 * row_flops * blocks,
    )
    halo = exchange(parts)
    state, low, early, table, cols = call(
        prepare_kernel,
        "prepare",
        whole([exports, positions], SMEM)
        + whole([in_hbm(live_blocks), in_hbm(col_slot.T)], pl.ANY)
        + whole([in_vmem(tracers), in_vmem(transport)]),
        [
            state_type,
            low_type,
            kept((offered, slots, block, block), BF16),
            (SMEM((TABLE,), jnp.int32), SMEM),
            (SMEM((slots, blocks), jnp.int32), SMEM),
        ],
        scratch=[
            SMEM((regions,), jnp.int32),
            SMEM((blocks,), jnp.int32),
            SMEM((offered,), jnp.int32),
            pltpu.SemaphoreType.DMA((2,)),
        ],
        flops=row_flops * blocks,
        moved=8 << 20,
    )
    turned = None
    staging = [VMEM((2, slots, block, block), BF16)] * 2
    scalars = whole([cols, table], SMEM)
    tracer_rows = [in_vmem(inverse), vmax.reshape(1, -1), half_sat.reshape(1, -1)]
    for cycle in range(CYCLES):
        for step in range(2):
            exported, *parts = call(
                export_kernel,
                "export_step",
                scalars + whole([early, low, state, *halo]),
                [kept((offered, width, block), F32)] + sends,
                scratch=[ext],
                flops=row_flops * offered,
            )
            arriving = exchange(parts)
            first = turned is None
            state, low, *more = call(
                functools.partial(rest_kernel, first),
                "rest_step",
                scalars
                + [(in_vmem(transport) if first else turned, VMEM)]
                + whole([low, state, *halo, exported]),
                [state_type, low_type]
                + ([kept((blocks - offered, *transport.shape[1:]), BF16)] if first else []),
                scratch=[ext] + (staging if first else []),
                flops=row_flops * blocks,
            )
            if first:
                (turned,) = more
            halo = arriving
        state, part = call(
            whole_kernel,
            "whole_step",
            scalars + whole([early, turned, low, state, *halo]),
            [state_type, sent((blocks, block), F32)],
            scratch=[ext],
            flops=row_flops * blocks,
        )
        operands = [(table, SMEM)] + whole([state, *tracer_rows, *across(part)])
        if cycle == CYCLES - 1:
            (out,) = call(
                functools.partial(implicit_kernel, "last", peers),
                "last_mix",
                operands,
                [(jax.ShapeDtypeStruct((width, rows), F32), pl.ANY)],
                scratch=[VMEM((width, rows), F32), pltpu.SemaphoreType.DMA((4,))],
                flops=row_flops * blocks // slots,
            )
            return out
        halo = exchange(
            call(
                functools.partial(implicit_kernel, "export", peers),
                "export_mix",
                operands,
                sends,
                scratch=[VMEM((offered, width, block), BF16), VMEM((blocks, block), F32)],
                flops=row_flops * offered // slots,
            )
        )
        state, low = call(
            functools.partial(implicit_kernel, "rest", peers),
            "rest_mix",
            operands,
            [state_type, low_type],
            flops=row_flops * blocks // slots,
        )


def solution(mesh):
    in_specs = (
        P("tracer", "region"),
        P("region", None, None, None),
        P("region", None),
        P("region", None),
        P(),
        P(),
        P("region", None, None),
        P("tracer"),
        P("tracer"),
    )
    out_specs = P("tracer", "region")
    return jax.shard_map(
        on_device, mesh=mesh, in_specs=in_specs, out_specs=out_specs, check_vma=False
    )
```

```python
import functools

import jax
import jax.numpy as jnp
from jax import lax
from jax.experimental import pallas as pl
from jax.experimental.pallas import tpu as pltpu
from jax.sharding import PartitionSpec as P

NTR = 256
LEVPAD = 64
LEVELS = 50
CYCLES = 2
OFFSETS = (-2, -1, 1, 2)

EXPORTS, SENDS, LINKS, REST, LIVE, COUNT, SPARE, TABLE = 0, 16, 48, 64, 100, 101, 120, 136

VMEM = pltpu.VMEM
SMEM = pltpu.SMEM
F32 = jnp.float32
BF16 = jnp.bfloat16


def from_behind(value, axis, distance):
    n = lax.axis_size(axis)
    route = [((i - distance) % n, i) for i in range(n)]
    return lax.ppermute(value, axis, route)


def link_neighbour(link, region):
    chip, core = region // 2 % 2, region % 2
    return (3 * chip, 3 - 3 * chip, 1 + core, 2 - core)[link]


def offset_of(which):
    return which - 2 + which // 2


def exchange(parts):
    n = lax.axis_size("region")
    arrived = []
    for link, part in enumerate(parts):
        route = [(r, (r + offset_of(link_neighbour(link, r))) % n) for r in range(n)]
        arrived.append(lax.ppermute(part, "region", route))
    return arrived


def in_vmem(value):
    return pltpu.with_memory_space_constraint(value, VMEM)


def spec(space):
    return pl.BlockSpec(memory_space=space)


def in_hbm(value):
    return pltpu.with_memory_space_constraint(value, pltpu.HBM)


def call(kernel, name, args, outs, scratch=(), flops=0, moved=1 << 20):
    return pl.pallas_call(
        kernel,
        in_specs=[spec(s) for _, s in args],
        out_specs=[spec(s) for _, s in outs],
        out_shape=[o for o, _ in outs],
        scratch_shapes=list(scratch),
        compiler_params=pltpu.CompilerParams(vmem_limit_bytes=12 << 20),
        cost_estimate=pl.CostEstimate(flops=flops, bytes_accessed=moved, transcendentals=0),
        name=name,
    )(*[v for v, _ in args])


def kept(shape, dtype):
    return (VMEM(shape, dtype), VMEM)


def sent(shape, dtype):
    return (jax.ShapeDtypeStruct(shape, dtype), VMEM)


def whole(values, space=VMEM):
    return [(v, space) for v in values]


def row_mask(block, live, shape):
    level = lax.rem(lax.broadcasted_iota(jnp.int32, shape, 1), LEVPAD)
    limit = jnp.where(block < live, LEVELS, 0)
    return jnp.where(level < limit, 1.0, 0.0).astype(F32)


def fetch(pairs, sems):
    copies = [pltpu.make_async_copy(a, b, sems.at[i]) for i, (a, b) in enumerate(pairs)]
    for copy in copies:
        copy.start()
    return copies


def read_position(positions, link, k):
    regions = positions.shape[2]
    mine = lax.axis_index("region")
    which = link_neighbour(link, mine)
    partner = lax.rem(mine + offset_of(which) + regions, regions)
    return positions[3 - which, k, partner]


def first_kernel(block, export_rows, send_pos, tracers, *refs):
    near, reach = send_pos.shape[:2]
    sends, (exports, positions, landed, sems) = refs[:near], refs[near:]
    for copy in fetch([(tracers, landed), (export_rows, exports), (send_pos, positions)], sems):
        copy.wait()
    for link in range(near):
        for k in range(reach):
            row = exports[0, read_position(positions, link, k)]
            columns = pl.ds(pl.multiple_of(row * block, block), block)
            sends[link][k] = landed[:, columns].astype(BF16)


def write_table(table, exported, again, set_of_offered, positions, wet, blocks, first, places):
    near, reach = positions.shape[:2]
    offered = len(exported)
    free = jnp.int32(0)
    for e, row in enumerate(exported):
        table[EXPORTS + e] = row
        places[jnp.minimum(free, offered - 1)] = jnp.int32(EXPORTS + e)
        free = free + again[e].astype(jnp.int32)
    for e in reversed(range(offered)):
        first[exported[e]] = jnp.int32(e)
    mine = lax.axis_index("region")
    for link in range(near):
        table[LINKS + link] = link_neighbour(link, mine)
        for k in range(reach):
            place = read_position(positions, link, k)
            table[SENDS + link * reach + k] = first[table[EXPORTS + place]]
    table[LIVE] = wet
    n = jnp.int32(0)
    count = jnp.int32(0)
    for b in range(blocks):
        other = 1 - jnp.bitwise_and(lax.shift_right_logical(set_of_offered, jnp.int32(b)), 1)
        place = jnp.where(n < free, places[jnp.minimum(n, offered - 1)], REST + n - free)
        table[jnp.where(other == 1, place, TABLE - 1)] = jnp.int32(b)
        count = count + jnp.where(b < wet, other, 0)
        n = n + other
    table[COUNT] = jnp.maximum(count - free, 0)


def prepare_kernel(
    exports,
    positions,
    live,
    col_slot,
    tracers,
    transport,
    state,
    low,
    early,
    table,
    cols,
    lives,
    first,
    places,
    sems,
):
    blocks, slots, block, _ = transport.shape
    offered = exports.shape[1]
    small = fetch([(live, lives), (col_slot, cols)], sems)
    exported = [exports[0, e] for e in range(offered)]
    again = []
    set_of_offered = jnp.int32(0)
    for row in exported:
        bit = lax.shift_left(jnp.int32(1), row)
        again.append(jnp.bitwise_and(set_of_offered, bit) != 0)
        set_of_offered = jnp.bitwise_or(set_of_offered, bit)

    small[0].wait()
    wet = lives[lax.axis_index("region")]
    write_table(table, exported, again, set_of_offered, positions, wet, blocks, first, places)
    for b in range(blocks):
        value = tracers[:, b * block : (b + 1) * block]
        state[b] = value
        low[b] = value.astype(BF16)
    for e in range(offered):
        b = table[EXPORTS + e]
        for s in range(slots):
            early[e, s] = transport[b, s].T
    small[1].wait()


def fill(ext, low, halo, table):
    blocks = low.shape[0]
    reach = halo[0].shape[0]
    ext[:blocks] = low[...]
    for link, part in enumerate(halo):
        ext[pl.ds(blocks + table[LINKS + link] * reach, reach)] = part[...]


def flux_of(b, cols, weights, ext):
    picked = jnp.concatenate([ext[cols[s, b]] for s in range(cols.shape[0])], axis=1)
    return jnp.dot(picked, weights, preferred_element_type=F32)


def stacked(rows):
    slots, block, _ = rows.shape
    return rows[...].reshape(slots * block, block)


def for_rest(table, rest, one, dry):
    def group_of(size, start):
        def several(i, carry):
            for u in range(size):
                one(start + i * size + u)
            return carry

        return several

    count = table[COUNT]
    left = lax.rem(count, 8)
    eights = lax.div(count, 8) + jnp.where(left > 4, 1, 0)
    fours = jnp.where(jnp.logical_and(left > 0, left <= 4), 1, 0)
    lax.fori_loop(0, eights, group_of(8, 0), 0)
    lax.fori_loop(0, fours, group_of(4, 8 * eights), 0)

    def dry_one(i, carry):
        dry(i)
        return carry

    lax.fori_loop(8 * eights + 4 * fours, rest, dry_one, 0)


def tracer_weights(width):
    first = lax.axis_index("tracer") * width
    ids = (first + lax.broadcasted_iota(jnp.int32, (width, 1), 0)).astype(F32)
    return 1.0 + 8.0 * ids / (NTR - 1)


def shade_part(state, weights):
    return jnp.sum(weights * state * state, axis=0, keepdims=True)


def export_kernel(cols, table, early, low, state, *refs):
    near = len(OFFSETS)
    halo, exported, sends, ext = refs[:near], refs[near], refs[near + 1 : -1], refs[-1]
    fill(ext, low, halo, table)
    for e in range(exported.shape[0]):
        b = table[EXPORTS + e]
        value = state[b] + flux_of(b, cols, stacked(early.at[e]), ext)
        exported[e] = row_mask(b, table[LIVE], value.shape) * value
    reach = sends[0].shape[0]
    for link in range(near):
        for k in range(reach):
            sends[link][k] = exported[table[SENDS + link * reach + k]].astype(BF16)


def rest_kernel(first, cols, table, weights, low, state, *refs):
    near = len(OFFSETS)
    halo, exported, refs = refs[:near], refs[near], refs[near + 1 :]
    offered = exported.shape[0]
    rest = state.shape[0] - offered
    if first:
        new_state, new_low, turned, ext, *fresh = refs
        quads = jnp.maximum(lax.div(table[COUNT] + 3, 4), 1)
    else:
        new_state, new_low, ext = refs
    fill(ext, low, halo, table)

    def put(b, value):
        new_state[b] = value
        new_low[b] = value.astype(BF16)

    for e in range(offered):
        put(table[EXPORTS + e], exported[e])

    def one(i, rows):
        b = table[REST + i]
        value = state[b] + flux_of(b, cols, rows, ext)
        put(b, row_mask(b, table[LIVE], value.shape) * value)

    def dry(i):
        put(table[REST + i], jnp.zeros(state.shape[1:], F32))

    if not first:
        for_rest(table, rest, lambda i: one(i, stacked(weights.at[i])), dry)
        return

    group = fresh[0].shape[0]

    def turn(start, there):
        for i in range(group):
            b = table[REST + start + i]
            for s in range(weights.shape[1]):
                tile = weights[b, s].T
                turned[start + i, s] = tile
                there[i, s] = tile

    def compute(start, there):
        for i in range(group):
            one(start + i, stacked(there.at[i]))

    def several(g, carry):
        start = 2 * g * group
        compute(start, fresh[0])
        turn(start + group, fresh[1])
        compute(start + group, fresh[1])
        turn(start + 2 * group, fresh[0])
        return carry

    turn(0, fresh[0])
    lax.fori_loop(0, quads - 1, several, 0)
    last = 2 * group * (quads - 1)
    compute(last, fresh[0])
    turn(last + group, fresh[1])
    compute(last + group, fresh[1])

    def dry_one(i, carry):
        dry(i)
        return carry

    lax.fori_loop(2 * group * quads, rest, dry_one, 0)


def whole_kernel(cols, table, early, turned, low, state, *refs):
    near = len(OFFSETS)
    halo, (new_state, part, ext) = refs[:near], refs[near:]
    fill(ext, low, halo, table)
    weights = tracer_weights(state.shape[1])

    def one(b, rows):
        value = state[b] + flux_of(b, cols, rows, ext)
        value = row_mask(b, table[LIVE], value.shape) * value
        new_state[b] = value
        part[pl.ds(b, 1), :] = shade_part(value, weights)

    for e in range(early.shape[0]):
        one(table[EXPORTS + e], stacked(early.at[e]))

    def dry(i):
        b = table[REST + i]
        new_state[b] = jnp.zeros(state.shape[1:], F32)
        part[pl.ds(b, 1), :] = jnp.zeros((1, part.shape[1]), F32)

    for_rest(table, turned.shape[0], lambda i: one(table[REST + i], stacked(turned.at[i])), dry)


def column_of(row):
    n = row.shape[1]
    there = lax.broadcasted_iota(jnp.int32, (n, n), 0) == lax.broadcasted_iota(jnp.int32, (n, n), 1)
    return jnp.sum(jnp.where(there, row, 0.0), axis=1, keepdims=True)


def uptake_kernel(state, vmax_row, half_row, uptakes):
    vmax = column_of(vmax_row[...])
    half_sat = column_of(half_row[...])
    for b in range(state.shape[0]):
        uptakes[b] = uptake_of(state[b], vmax, half_sat)


def uptake_of(value, vmax, half_sat):
    return vmax * value / (half_sat + jnp.abs(value))


def mixed_block(value, shade, uptake, inverse):
    level = lax.rem(lax.broadcasted_iota(jnp.int32, shade.shape, 1), LEVPAD)
    light = jnp.exp(-level.astype(F32) / LEVELS)
    pre = (value - light / (1.0 + shade) * uptake).astype(BF16)
    return lax.dot_general(pre, inverse, (((1,), (1,)), ((), ())), preferred_element_type=F32)


def implicit_kernel(kind, peers, table, state, inverse, *refs):
    if kind == "last":
        uptakes, *refs = refs
    else:
        vmax, half_sat = column_of(refs[0][...]), column_of(refs[1][...])
        refs = refs[2:]
    parts, outs = refs[:peers], refs[peers:]
    total = parts[0][...]
    for p in parts[1:]:
        total = total + p[...]
    total = total / (16.0 * NTR)
    if kind == "export":
        *sends, mixes, shade = outs
        shade[...] = total
        for e in range(mixes.shape[0]):
            b = table[EXPORTS + e]
            mixed = mixed_block(
                state[b], shade[pl.ds(b, 1), :], uptake_of(state[b], vmax, half_sat), inverse[b]
            )
            mixes[e] = (row_mask(b, table[LIVE], mixed.shape) * mixed).astype(BF16)
        reach = sends[0].shape[0]
        for link, part in enumerate(sends):
            for k in range(reach):
                part[k] = mixes[table[SENDS + link * reach + k]]
        return
    blocks, _, block = state.shape
    copies = []
    for b in range(blocks):
        uptake = uptakes[b] if kind == "last" else uptake_of(state[b], vmax, half_sat)
        mixed = mixed_block(state[b], total[b : b + 1], uptake, inverse[b])
        mixed = row_mask(b, table[LIVE], mixed.shape) * mixed
        if kind == "rest":
            outs[0][b] = mixed
            outs[1][b] = mixed.astype(BF16)
        else:
            out, made, sems = outs
            made[:, b * block : (b + 1) * block] = mixed
            each = blocks // sems.shape[0]
            if (b + 1) % each == 0:
                part = pl.ds((b + 1 - each) * block, each * block)
                copy = pltpu.make_async_copy(made.at[:, part], out.at[:, part], sems.at[b // each])
                copy.start()
                copies.append(copy)
    for copy in copies:
        copy.wait()


def on_device(
    tracers, transport, col_slot, export_rows, send_pos, live_blocks, inverse, vmax, half_sat
):
    width, rows = tracers.shape
    blocks, slots = col_slot.shape
    block = rows // blocks
    near, reach = send_pos.shape[1:]
    offered = export_rows.shape[1]
    peers = lax.axis_size("tracer")
    row_flops = 2 * width * slots * block * block

    sends = [sent((reach, width, block), BF16)] * near
    ext = VMEM((blocks + near * reach, width, block), BF16)
    state_type = kept((blocks, width, block), F32)
    low_type = kept((blocks, width, block), BF16)

    def across(part):
        return [part] + [lax.ppermute(part, "tracer", [(i, i ^ d) for i in range(peers)]) for d in (1, 3, 2)]

    regions = send_pos.shape[0]
    *parts, exports, positions = call(
        functools.partial(first_kernel, block),
        "offer_first",
        whole([in_hbm(export_rows), in_hbm(send_pos.transpose(1, 2, 0)), in_hbm(tracers)], pl.ANY),
        sends
        + [
            (SMEM((1, offered), jnp.int32), SMEM),
            (SMEM((near, reach, regions), jnp.int32), SMEM),
        ],
        scratch=[VMEM((width, rows), F32), pltpu.SemaphoreType.DMA((3,))],
        flops=12 * row_flops * blocks,
    )
    halo = exchange(parts)
    state, low, early, table, cols = call(
        prepare_kernel,
        "prepare",
        whole([exports, positions], SMEM)
        + whole([in_hbm(live_blocks), in_hbm(col_slot.T)], pl.ANY)
        + whole([in_vmem(tracers), in_vmem(transport)]),
        [
            state_type,
            low_type,
            kept((offered, slots, block, block), BF16),
            (SMEM((TABLE,), jnp.int32), SMEM),
            (SMEM((slots, blocks), jnp.int32), SMEM),
        ],
        scratch=[
            SMEM((regions,), jnp.int32),
            SMEM((blocks,), jnp.int32),
            SMEM((offered,), jnp.int32),
            pltpu.SemaphoreType.DMA((2,)),
        ],
        flops=row_flops * blocks,
        moved=8 << 20,
    )
    turned = None
    staging = [VMEM((2, slots, block, block), BF16)] * 2
    scalars = whole([cols, table], SMEM)
    tracer_rows = [vmax.reshape(1, -1), half_sat.reshape(1, -1)]
    for cycle in range(CYCLES):
        for step in range(2):
            exported, *parts = call(
                export_kernel,
                "export_step",
                scalars + whole([early, low, state, *halo]),
                [kept((offered, width, block), F32)] + sends,
                scratch=[ext],
                flops=row_flops * offered,
            )
            arriving = exchange(parts)
            first = turned is None
            state, low, *more = call(
                functools.partial(rest_kernel, first),
                "rest_step",
                scalars
                + [(in_vmem(transport) if first else turned, VMEM)]
                + whole([low, state, *halo, exported]),
                [state_type, low_type]
                + ([kept((blocks - offered, *transport.shape[1:]), BF16)] if first else []),
                scratch=[ext] + (staging if first else []),
                flops=row_flops * blocks,
            )
            if first:
                (turned,) = more
            halo = arriving
        state, part = call(
            whole_kernel,
            "whole_step",
            scalars + whole([early, turned, low, state, *halo]),
            [state_type, sent((blocks, block), F32)],
            scratch=[ext],
            flops=row_flops * blocks,
        )
        shades = across(part)
        uptakes = tracer_rows
        if cycle == CYCLES - 1:
            uptakes = call(
                uptake_kernel, "uptake", whole([state, *tracer_rows]), [state_type], moved=2 << 20
            )
        operands = [(table, SMEM)] + whole([state, in_vmem(inverse), *uptakes, *shades])
        if cycle == CYCLES - 1:
            (out,) = call(
                functools.partial(implicit_kernel, "last", peers),
                "last_mix",
                operands,
                [(jax.ShapeDtypeStruct((width, rows), F32), pl.ANY)],
                scratch=[VMEM((width, rows), F32), pltpu.SemaphoreType.DMA((4,))],
                flops=row_flops * blocks // slots,
            )
            return out
        halo = exchange(
            call(
                functools.partial(implicit_kernel, "export", peers),
                "export_mix",
                operands,
                sends,
                scratch=[VMEM((offered, width, block), BF16), VMEM((blocks, block), F32)],
                flops=row_flops * offered // slots,
            )
        )
        state, low = call(
            functools.partial(implicit_kernel, "rest", peers),
            "rest_mix",
            operands,
            [state_type, low_type],
            flops=row_flops * blocks // slots,
        )


def solution(mesh):
    in_specs = (
        P("tracer", "region"),
        P("region", None, None, None),
        P("region", None),
        P("region", None),
        P(),
        P(),
        P("region", None, None),
        P("tracer"),
        P("tracer"),
    )
    out_specs = P("tracer", "region")
    return jax.shard_map(
        on_device, mesh=mesh, in_specs=in_specs, out_specs=out_specs, check_vma=False
    )
```
